32 devices in a mesh: dp: 4 (over y, x), seq: 4 (over z), mp: 2 (over core).
Axes of the slice: x: 2, y: 2, z: 4, core: 2. Of those that a mesh axis runs over, the one named last changes fastest.
Arguments:
- hidden_states: bfloat16 [2048, 2048], P(('dp', 'seq')), may hold values from -6 to 6
- embeddings: bfloat16 [2048, 2048], P(('dp', 'seq')), may hold values from -6 to 6
- norm_gain: float32 [4096], replicated, may hold values from 0.1 to 1.9
- input_weights: bfloat16 [4096, 3, 2, 2048], P('dp', None, 'mp', 'seq'), may hold values from -0.09375 to 0.09375
- adapter_down: bfloat16 [4096, 384], P(('seq', 'mp')), may hold values from -0.09375 to 0.09375
- adapter_up: bfloat16 [3, 128, 2, 2048], P(None, None, 'mp', 'seq'), may hold values from -0.5 to 0.5
- output_weights: bfloat16 [2, 2048, 2048], P('mp', 'seq', 'dp'), may hold values from -3 to 3
- own_keys: bfloat16 [4, 4096, 4096], P('dp', 'seq', 'mp'), may hold values from -164 to 164
- own_values: bfloat16 [4, 4096, 4096], P('dp', 'seq', 'mp'), may hold values from -6 to 6
- shared_keys: bfloat16 [2, 512, 4096], P(None, 'seq', 'mp'), may hold values from -164 to 164
- shared_values: bfloat16 [2, 512, 4096], P(None, 'seq', 'mp'), may hold values from -6 to 6
- cached_lengths: int32 [4], P('dp'), may hold values from 1 to 4096, 8192 in all
- prompt_group: int32 [4], P('dp'), may hold values from 0 to 1
- slot_pages: int32 [4, 64], P('dp', 'seq'), may hold values from 0 to 63, as said below
- padding_mask: int32 [2048], P(('dp', 'seq', 'mp')), may hold values from 0 to 1, as said below
Outputs:
- mixed: bfloat16 [2048, 2048], P(('dp', 'seq', 'mp'))
The draws below stay inside these ranges and needn't reach their ends.
Inputs may be any that keep to these rules, and one draw needn't show every extreme that they name: `slot_pages`: row r maps the 64 page slots of request r one to one onto its pages: slot u holds page (u + c * 16) mod 64 for a whole number c of request r; page p holds own positions p * 64 to p * 64 + 63. `padding_mask`: within each request's 512 tokens the ones come first, then the zeros; at least 128 ones.
All inputs are finite; a program needn't handle non-finite values. No bound on the sum of `cached_lengths` on one device may be relied on, other than what follows from the above.
Results may differ from the reference program's by a relative error of at most 0.025.
The reference program's roundings to bfloat16 on the way count: a program that leaves them out, or rounds other values in their place, can miss the bound.
Values may be sent and summed in bfloat16 or wider, within the bound.
No kernel may reach another device: no remote copies, remote signals or barrier semaphores. Data moves between devices by JAX's collectives and lax.ppermute only.
A program may use at most 128 MiB of HBM per device.

```python
import math
import jax
import jax.numpy as jnp
import numpy as np
from jax import lax

D = 2048
HEADS = 32
HD = 128
RANK = 128
NEW = 512
PAGE = 64
NGROUPS = 2
OWN_DEV = 1024
SHARED_DEV = 128
D_IN = 4096
HEADS_MP = 16
REQS = 4
TOKENS = 2048
OWN_MAX = 4096
SHARED = 512
PAGES = 64
PAGES_DEV = 16
N_SEQ = 4
N_MP = 2


def spiked_keys(key, shape):
    base_key = jax.random.fold_in(key, 0)
    values = jnp.clip(jax.random.normal(base_key, shape, jnp.float32), -6.0, 6.0)
    return values.astype(jnp.bfloat16)


def draw_own_keys(key, part):
    return spiked_keys(jax.random.fold_in(key, 11), (REQS, OWN_MAX, HEADS * HD))


def draw_shared_keys(key, part):
    return spiked_keys(jax.random.fold_in(key, 13), (NGROUPS, SHARED, HEADS * HD))


def draw_prompt_group(key, part):
    groups = jax.random.randint(jax.random.fold_in(key, 17), (REQS,), 0, NGROUPS)
    return groups.at[0].set(0).at[1].set(1).astype(jnp.int32)


def draw_slot_pages(key, part):
    shifts = jax.random.randint(jax.random.fold_in(key, 19), (REQS, 1), 0, PAGES // PAGES_DEV)
    pages = (jnp.arange(PAGES, dtype=jnp.int32)[None, :] + shifts * PAGES_DEV) % PAGES
    return pages.astype(jnp.int32)


def draw_padding_mask(key, part):
    counts = jax.random.randint(jax.random.fold_in(key, 23), (REQS,), NEW // 4, NEW + 1)
    counts = counts.at[0].set(NEW).at[REQS - 1].set(NEW // 2)
    places = jnp.arange(NEW, dtype=jnp.int32)
    return (places[None, :] < counts[:, None]).astype(jnp.int32).reshape(TOKENS)


def steps_of(rng, shape, shards, least, largest):
    loudness, own = 1.0, jax.random.fold_in(rng, 6)
    for position, blocks in shards:
        draws = jnp.exp(jax.random.uniform(jax.random.fold_in(own, position), (blocks,), jnp.float32, least / len(shards), largest / len(shards)))
        loudness = loudness * jnp.repeat(draws, shape[position] // blocks).reshape([-1 if axis == position else 1 for axis in range(len(shape))])
    return loudness


def profile(count, total, reach, lean):
    weights = [(1 << 20) // math.isqrt(rank ** lean) + 1 for rank in range(2, count + 1)]
    surplus, given = total - reach - (count - 1), [1] * (count - 1)
    while surplus > 0:
        free = [i for i in range(count - 1) if given[i] < reach]
        mass, remaining = sum([weights[i] for i in free]), surplus
        for i in free:
            addition = min(reach - given[i], max(1, remaining * weights[i] // mass), surplus)
            given[i] = given[i] + addition
            surplus = surplus - addition
    return np.array([reach] + given)


def ragged(own_key, count, total, limit, skew):
    if count == 2:
        one = jax.random.randint(own_key, (), max(1, total - limit), min(limit, total - 1) + 1)
        return jnp.stack([one, total - one])
    lengths = jnp.asarray(profile(count, total, limit, skew), jnp.int32)
    couples = (count - 1) // 2
    giver, receiver = lengths[1:1 + 2 * couples:2], lengths[2:2 + 2 * couples:2]
    room = jnp.minimum(giver - 1, limit - receiver)
    passed = jax.random.randint(jax.random.fold_in(own_key, 1), (couples,), 0, 1 << 20) % (room + 1)
    lengths = lengths.at[1:1 + 2 * couples:2].set(giver - passed).at[2:2 + 2 * couples:2].set(receiver + passed)
    return lengths[jax.random.permutation(jax.random.fold_in(own_key, 2), count)]


def bell_draw(rng, shape, width, reach, shards=(), kind=jnp.bfloat16):
    level = steps_of(rng, shape, shards, -0.22, 0.18) if shards else 1.0
    values = jax.random.normal(rng, shape, jnp.float32) * width * level
    return jnp.minimum(jnp.maximum(values, -reach), reach).astype(kind)


def setup_inputs(seed: int = 0) -> dict:
    streams_of = jax.random.split(jax.random.key(seed), 16)
    return {
        "hidden_states": bell_draw(streams_of[0], (TOKENS, D), 1.0, 6.0, ((0, 16),)),
        "embeddings": bell_draw(streams_of[1], (TOKENS, D), 1.0, 6.0, ((0, 16),)),
        "norm_gain": jnp.clip(1.0 + 0.18 * jax.random.normal(streams_of[2], (D_IN,), jnp.float32), 0.1, 1.9),
        "input_weights": bell_draw(streams_of[3], (D_IN, 3, N_MP, HEADS_MP * HD), D_IN ** -0.5, 0.09375, ((0, 4), (2, 2), (3, 4))),
        "adapter_down": bell_draw(streams_of[4], (D_IN, 3 * RANK), D_IN ** -0.5, 0.09375, ((0, 8),)),
        "adapter_up": bell_draw(streams_of[5], (3, RANK, N_MP, HEADS_MP * HD), RANK ** -0.5, 0.5, ((2, 2), (3, 4))),
        "output_weights": bell_draw(streams_of[6], (N_MP, HEADS_MP * HD, D), (12 / (HEADS * HD) ** 0.5), 3.0, ((0, 2), (1, 4), (2, 4))),
        "own_keys": draw_own_keys(jax.random.fold_in(streams_of[15], 71), 0),
        "own_values": bell_draw(streams_of[8], (REQS, OWN_MAX, HEADS * HD), 1.0, 6.0, ((0, 4), (1, 4), (2, 2))),
        "shared_keys": draw_shared_keys(jax.random.fold_in(streams_of[15], 71), 0),
        "shared_values": bell_draw(streams_of[10], (NGROUPS, SHARED, HEADS * HD), 1.0, 6.0, ((1, 4), (2, 2))),
        "cached_lengths": ragged(streams_of[11], REQS, REQS * OWN_MAX // 2, OWN_MAX, 2).astype(jnp.int32),
        "prompt_group": draw_prompt_group(jax.random.fold_in(streams_of[15], 71), 0),
        "slot_pages": draw_slot_pages(jax.random.fold_in(streams_of[15], 71), 0),
        "padding_mask": draw_padding_mask(jax.random.fold_in(streams_of[15], 71), 0),
    }


eps = 1e-05
neg_fill = -1e+30

def to_narrow(values):
    return lax.optimization_barrier(values.astype(jnp.bfloat16))

def normalize(hidden_rows, embed_rows, norm_gain):
    joined = jnp.concatenate([hidden_rows, embed_rows], axis=1).astype(jnp.float32)
    factor = lax.rsqrt(lax.optimization_barrier(jnp.mean(joined * joined, axis=1, keepdims=True)) + eps)
    return to_narrow(joined * factor * norm_gain)

def block_partial(queries, keys, values, usable):
    scaling = 1.0 / math.sqrt(queries.shape[2])
    scores = jnp.einsum('ihd,jhd->hij', queries.astype(jnp.float32), keys.astype(jnp.float32)) * scaling
    scores = jnp.where(usable[None], scores, neg_fill)
    peak_score = lax.optimization_barrier(jnp.max(scores, axis=2))
    exponent = jnp.exp(scores - peak_score[:, :, None])
    totals = lax.optimization_barrier(jnp.sum(exponent, axis=2))
    narrow = to_narrow(exponent)
    weighted = jnp.einsum('hij,jhd->ihd', narrow.astype(jnp.float32), values.astype(jnp.float32))
    weighted = weighted / jnp.transpose(totals)[:, :, None]
    return (to_narrow(weighted), jnp.transpose(peak_score), jnp.transpose(totals))

def fold_partials(outputs, peak_scores, totals):
    highest = lax.optimization_barrier(jnp.max(peak_scores, axis=0))
    weight = totals * jnp.exp(peak_scores - highest)
    return lax.optimization_barrier(jnp.sum(weight[..., None] * outputs, axis=0)) / lax.optimization_barrier(jnp.sum(weight, axis=0))[..., None]

def reference(hidden_states, embeddings, norm_gain, input_weights, adapter_down, adapter_up, output_weights, own_keys, own_values, shared_keys, shared_values, cached_lengths, prompt_group, slot_pages, padding_mask):
    flat_weights = input_weights.reshape(D_IN, 3 * HEADS * HD)
    flat_up = adapter_up.reshape(3, RANK, HEADS * HD).astype(jnp.float32)
    flat_out = output_weights.reshape(HEADS * HD, D)

    def one_request(request_items):
        hidden_rows, embed_rows, keys_own, values_own, length, group_index, pages, padding = request_items
        normed = normalize(hidden_rows, embed_rows, norm_gain)
        low_rank = to_narrow(jnp.dot(normed, adapter_down, preferred_element_type=jnp.float32))
        base_terms = jnp.dot(normed, flat_weights, preferred_element_type=jnp.float32).reshape(NEW, 3, HEADS * HD)
        lifted = jnp.einsum('ipr,prc->ipc', low_rank.reshape(NEW, 3, RANK).astype(jnp.float32), flat_up)
        projected = to_narrow(base_terms + lifted)
        queries = projected[:, 0].reshape(NEW, HEADS, HD)
        keys_new = projected[:, 1].reshape(NEW, HEADS, HD)
        values_new = projected[:, 2].reshape(NEW, HEADS, HD)
        positions = jnp.repeat(pages, PAGE, total_repeat_length=OWN_MAX) * PAGE + jnp.arange(OWN_MAX, dtype=jnp.int32) % PAGE
        own_usable = positions < length
        shared_k = lax.dynamic_index_in_dim(shared_keys, group_index, 0, keepdims=False)
        shared_v = lax.dynamic_index_in_dim(shared_values, group_index, 0, keepdims=False)

        def one_shard(shard_items):
            keys_part, values_part, usable_part, shared_kpart, shared_vpart = shard_items
            keys_all = jnp.concatenate([keys_part, shared_kpart], axis=0).reshape(-1, HEADS, HD)
            values_all = jnp.concatenate([values_part, shared_vpart], axis=0).reshape(-1, HEADS, HD)
            usable = jnp.concatenate([usable_part, jnp.ones((SHARED_DEV,), dtype=jnp.bool_)])[None, :]
            return block_partial(queries, keys_all, values_all, usable)
        shard_outputs, shard_peaks, shard_totals = lax.map(one_shard, (keys_own.reshape(N_SEQ, OWN_DEV, HEADS * HD), values_own.reshape(N_SEQ, OWN_DEV, HEADS * HD), own_usable.reshape(N_SEQ, OWN_DEV), shared_k.reshape(N_SEQ, SHARED_DEV, HEADS * HD), shared_v.reshape(N_SEQ, SHARED_DEV, HEADS * HD)))
        places = jnp.arange(NEW, dtype=jnp.int32)
        causal = places[:, None] >= places[None, :]
        new_output, new_peak, new_total = block_partial(queries, keys_new, values_new, causal)
        outputs = jnp.concatenate([shard_outputs, new_output[None]], axis=0).astype(jnp.float32)
        peak_scores = jnp.concatenate([shard_peaks, new_peak[None]], axis=0)
        totals = jnp.concatenate([shard_totals, new_total[None]], axis=0)
        attended = to_narrow(fold_partials(outputs, peak_scores, totals)).reshape(NEW, HEADS * HD)
        product = jnp.dot(attended, flat_out, preferred_element_type=jnp.float32)
        return (padding.astype(jnp.float32)[:, None] * product).astype(jnp.bfloat16)
    result = lax.map(one_request, (hidden_states.reshape(REQS, NEW, D), embeddings.reshape(REQS, NEW, D), own_keys, own_values, cached_lengths, prompt_group, slot_pages, padding_mask.reshape(REQS, NEW)))
    return result.reshape(TOKENS, D)
```

```python
import functools
import math

import jax
import jax.numpy as jnp
from jax import lax
from jax.experimental import pallas as pl
from jax.experimental.pallas import tpu as pltpu
from jax.sharding import PartitionSpec as P

HD = 128
PAGE = 64
EPS = 1e-05
NEG = -1e30
STAT_ROWS = 16
VMEM_LIMIT = 56 * 1024 * 1024

SMEM = pltpu.MemorySpace.SMEM
F32 = jnp.float32
BF16 = jnp.bfloat16


def swap(count, k):
    return [(i, i ^ k) for i in range(count)]


def after(value, *earlier):
    return lax.optimization_barrier((value, *earlier))[0]


def last(pieces):
    return [piece[0] for piece in pieces[-2:]]


def params():
    return pltpu.CompilerParams(vmem_limit_bytes=VMEM_LIMIT)


def cost(flops, moved, transcendentals=0):
    return pl.CostEstimate(flops=flops, bytes_accessed=moved, transcendentals=transcendentals)


def spread(x):
    count = lax.axis_size("seq")
    if count != 4:
        return [[lax.ppermute(x, "seq", swap(count, k))] for k in range(1, count)]
    outward = [(1, 0), (2, 3)]
    middle = [(1, 2), (2, 1)]
    near = lax.ppermute(x, "seq", swap(4, 1))
    across = lax.ppermute(x, "seq", middle)
    second_end = lax.ppermute(across, "seq", outward)
    second_middle = lax.ppermute(near, "seq", middle)
    third_end = lax.ppermute(second_middle, "seq", outward)
    return [[near], [second_end, second_middle], [third_end, across]]


def gather_dp(x):
    count = lax.axis_size("dp")
    if count != 4:
        return [(lax.all_gather(x, "dp", axis=0, tiled=True), None, 0)]
    half = x.shape[0] // 2
    top, bottom = x[:half], x[half:]
    top_1 = lax.ppermute(top, "dp", swap(4, 1))
    bottom_2 = lax.ppermute(bottom, "dp", swap(4, 2))
    top_2 = lax.ppermute(top, "dp", swap(4, 2))
    bottom_1 = lax.ppermute(bottom, "dp", swap(4, 1))
    top_3 = lax.ppermute(top_1, "dp", swap(4, 2))
    bottom_3 = lax.ppermute(bottom_2, "dp", swap(4, 1))
    return [
        (x, 0, 0),
        (top_1, 1, 0),
        (bottom_1, 1, half),
        (top_2, 2, 0),
        (bottom_2, 2, half),
        (top_3, 3, 0),
        (bottom_3, 3, half),
    ]


def gather_down(part):
    dp_count, seq_count = lax.axis_size("dp"), lax.axis_size("seq")
    rows = part.shape[0] // dp_count
    width = part.shape[1]
    own = lax.dynamic_slice_in_dim(part, lax.axis_index("dp") * rows, rows, 0)
    along = lax.all_gather(own, "seq", axis=0, tiled=True)
    if dp_count != 4:
        whole = lax.all_gather(along, "dp", axis=0, tiled=False)
    else:
        pieces = gather_dp(along)
        blocks = [along] + [
            jnp.concatenate([pieces[2 * k - 1][0], pieces[2 * k][0]], axis=0) for k in (1, 2, 3)
        ]
        index = lax.axis_index("dp")
        odd, high = (index & 1) == 1, (index & 2) == 2
        blocks = [jnp.where(odd, blocks[k ^ 1], blocks[k]) for k in range(4)]
        blocks = [jnp.where(high, blocks[k ^ 2], blocks[k]) for k in range(4)]
        whole = jnp.stack(blocks)
    other = lax.ppermute(whole, "mp", swap(2, 1))
    first = lax.axis_index("mp") == 0
    both = jnp.stack([jnp.where(first, whole, other), jnp.where(first, other, whole)])
    both = both.reshape(2, dp_count, seq_count, rows, width)
    return jnp.transpose(both, (2, 0, 1, 3, 4)).reshape(-1, width)


def norm_kernel(at, hidden_ref, embed_ref, gain_ref, out_ref):
    hidden = hidden_ref[...].astype(F32)
    embed = embed_ref[...].astype(F32)
    width = hidden.shape[1]
    squares = jnp.sum(hidden * hidden, axis=1, keepdims=True) + jnp.sum(
        embed * embed, axis=1, keepdims=True
    )
    factor = lax.rsqrt(squares / (2 * width) + EPS)

    @pl.when(at[2] == 0)
    def _():
        out_ref[...] = (hidden * factor * gain_ref[:, :width]).astype(BF16)

    @pl.when(at[2] != 0)
    def _():
        out_ref[...] = (embed * factor * gain_ref[:, width:]).astype(BF16)


def norm(at, hidden, embed, gain):
    return pl.pallas_call(
        norm_kernel,
        out_shape=jax.ShapeDtypeStruct(hidden.shape, BF16),
        in_specs=[pl.BlockSpec(memory_space=SMEM)] + [pl.BlockSpec(memory_space=pltpu.VMEM)] * 3,
        out_specs=pl.BlockSpec(memory_space=pltpu.VMEM),
        compiler_params=params(),
        name="norm",
    )(at, hidden, embed, gain)


def project_kernel(plan, at, *refs):
    seq_slots, pieces = plan
    refs = list(refs)
    mine = [[refs.pop(0) for _ in range(count)] for count in seq_slots]
    other = [[refs.pop(0) for _ in range(count)] for count in seq_slots]
    weights = [refs.pop(0) for _ in pieces]
    down_ref, up_ref, out_ref, joined = refs
    dp, seq, first, is_end = at[0], at[1], at[2] == 0, at[3] == 1
    rows, width = mine[0][0].shape

    def pick(candidates):
        if len(candidates) == 1:
            return candidates[0][...]
        return jnp.where(is_end, candidates[0][...], candidates[1][...])

    for k in range(len(seq_slots)):
        here, there = pick(mine[k]), pick(other[k])
        at_row = pl.ds(pl.multiple_of((seq ^ k) * rows, rows), rows)
        joined[at_row, :width] = jnp.where(first, here, there)
        joined[at_row, width:] = jnp.where(first, there, here)
    low = jnp.dot(joined[...], down_ref[...], preferred_element_type=F32).astype(BF16)
    total = jnp.dot(low, up_ref[...], preferred_element_type=F32)
    for (k, start, size, shard), ref in zip(pieces, weights):
        if k is None:
            columns = joined[...]
        else:
            begin = (dp ^ k) * shard + start
            columns = joined[:, pl.ds(pl.multiple_of(begin, size), size)]
        total += jnp.dot(columns, ref[...], preferred_element_type=F32)
    out_ref[...] = total.astype(BF16)


def project(at, mine, other, pieces, shard, down, up):
    rows = mine[0][0].shape[0] * len(mine)
    width = 2 * mine[0][0].shape[1]
    plan = (
        tuple(len(slot) for slot in mine),
        tuple((k, start, array.shape[0], shard) for array, k, start in pieces),
    )
    arrays = [x for slot in mine for x in slot] + [x for slot in other for x in slot]
    arrays += [array for array, _, _ in pieces] + [down, up]
    columns = up.shape[1]
    return pl.pallas_call(
        functools.partial(project_kernel, plan),
        out_shape=jax.ShapeDtypeStruct((rows, columns), BF16),
        in_specs=[pl.BlockSpec(memory_space=SMEM)]
        + [pl.BlockSpec(memory_space=pltpu.VMEM)] * len(arrays),
        out_specs=pl.BlockSpec(memory_space=pltpu.VMEM),
        scratch_shapes=[pltpu.VMEM((rows, width), BF16)],
        compiler_params=params(),
        cost_estimate=cost(2 * rows * width * (columns + HD), 2 * width * (rows + columns)),
        name="project",
    )(at, *arrays)


def finish_head(head, heads, weighted, peak, total, out_ref, stats):
    level = peak + jnp.log(total)
    high = level.astype(BF16).astype(F32)
    rest = level - high
    mid = rest.astype(BF16).astype(F32)
    stats[pl.ds(3 * head, 1), :] = high
    stats[pl.ds(3 * head + 1, 1), :] = mid
    stats[pl.ds(3 * head + 2, 1), :] = (rest - mid).astype(BF16).astype(F32)
    at_head = pl.ds(pl.multiple_of(head * HD, HD), HD)
    out_ref[at_head, :] = (weighted / total).astype(BF16)

    @pl.when(head == heads - 1)
    def _():
        out_ref[heads * HD :, :] = stats[...].astype(BF16)


def over_keys(left, right):
    return lax.dot_general(left, right, (((0,), (0,)), ((), ())), preferred_element_type=F32)


def scores_of(keys, queries):
    return lax.dot_general(keys, queries, (((1,), (1,)), ((), ())), preferred_element_type=F32)


def cache_kernel(heads, query_count, at, pages, *refs):
    query_refs = refs[:query_count]
    key_ref, value_ref, shared_key_ref, shared_value_ref, out_ref, stats = refs[query_count:]
    head = pl.program_id(0)

    @pl.when(head == 0)
    def _():
        stats[...] = jnp.zeros_like(stats)

    queries = query_refs[0][...]
    if query_count == 2:
        queries = jnp.where(at[3] == 1, queries, query_refs[1][...])
    scale = 1.0 / math.sqrt(HD)
    own = scores_of(key_ref[0], queries) * scale
    shared = scores_of(shared_key_ref[0], queries) * scale
    offset = lax.broadcasted_iota(jnp.int32, (PAGE, own.shape[1]), 0)
    masked = []
    for u in range(own.shape[0] // PAGE):
        usable = offset < at[4] - pages[u] * PAGE
        masked.append(jnp.where(usable, own[u * PAGE : (u + 1) * PAGE], NEG))
    own = jnp.concatenate(masked, axis=0)
    peak = jnp.maximum(
        jnp.max(own, axis=0, keepdims=True), jnp.max(shared, axis=0, keepdims=True)
    )
    own = jnp.exp(own - peak)
    shared = jnp.exp(shared - peak)
    total = jnp.sum(own, axis=0, keepdims=True) + jnp.sum(shared, axis=0, keepdims=True)
    weighted = over_keys(value_ref[0], own.astype(BF16)) + over_keys(
        shared_value_ref[0], shared.astype(BF16)
    )
    finish_head(head, heads, weighted, peak, total, out_ref, stats)


def cache_attention(at, pages, slot, queries, own_keys, own_values, shared_keys, shared_values):
    rows, width = queries[0].shape
    heads = width // HD
    slots, shared_slots = own_keys.shape[1], shared_keys.shape[1]

    def own_block(h, at, pages):
        return (0, 0, (at[1] ^ slot) * heads + h)

    def shared_block(h, at, pages):
        return (at[5], 0, (at[1] ^ slot) * heads + h)

    return pl.pallas_call(
        functools.partial(cache_kernel, heads, len(queries)),
        out_shape=jax.ShapeDtypeStruct((width + STAT_ROWS, rows), BF16),
        grid_spec=pltpu.PrefetchScalarGridSpec(
            num_scalar_prefetch=2,
            grid=(heads,),
            in_specs=[pl.BlockSpec((rows, HD), lambda h, at, pages: (0, h))] * len(queries)
            + [pl.BlockSpec((1, slots, HD), own_block)] * 2
            + [pl.BlockSpec((1, shared_slots, HD), shared_block)] * 2,
            out_specs=pl.BlockSpec((width + STAT_ROWS, rows), lambda h, at, pages: (0, 0)),
            scratch_shapes=[pltpu.VMEM((STAT_ROWS, rows), F32)],
        ),
        compiler_params=params(),
        cost_estimate=cost(
            8 * rows * width * (slots + shared_slots),
            4 * width * (slots + shared_slots),
            rows * heads * (slots + shared_slots),
        ),
        name="cache_attention",
    )(at, pages, *queries, own_keys, own_values, shared_keys, shared_values)


def new_kernel(heads, query_ref, key_ref, value_ref, out_ref, stats):
    head = pl.program_id(0)

    @pl.when(head == 0)
    def _():
        stats[...] = jnp.zeros_like(stats)

    scores = scores_of(key_ref[...], query_ref[...]) * (1.0 / math.sqrt(HD))
    places = lax.broadcasted_iota(jnp.int32, scores.shape, 0)
    tokens = lax.broadcasted_iota(jnp.int32, scores.shape, 1)
    scores = jnp.where(places <= tokens, scores, NEG)
    peak = jnp.max(scores, axis=0, keepdims=True)
    exponent = jnp.exp(scores - peak)
    total = jnp.sum(exponent, axis=0, keepdims=True)
    weighted = over_keys(value_ref[...], exponent.astype(BF16))
    finish_head(head, heads, weighted, peak, total, out_ref, stats)


def new_attention(queries, keys, values):
    rows, width = queries.shape
    heads = width // HD
    return pl.pallas_call(
        functools.partial(new_kernel, heads),
        out_shape=jax.ShapeDtypeStruct((width + STAT_ROWS, rows), BF16),
        grid=(heads,),
        in_specs=[pl.BlockSpec((rows, HD), lambda h: (0, h))] * 3,
        out_specs=pl.BlockSpec((width + STAT_ROWS, rows), lambda h: (0, 0)),
        scratch_shapes=[pltpu.VMEM((STAT_ROWS, rows), F32)],
        compiler_params=params(),
        cost_estimate=cost(8 * rows * rows * width, 8 * rows * width, rows * rows * heads),
        name="new_attention",
    )(queries, keys, values)


def merge_kernel(heads, blocks, at, *refs):
    parts = refs[: len(refs) - 3]
    keep_ref, give_ref, attended = refs[len(refs) - 3 :]
    base = heads * HD
    for h in range(heads):
        levels = []
        for part in parts:
            stats = part[base : base + STAT_ROWS, :].astype(F32)
            levels.append(
                stats[3 * h : 3 * h + 1] + (stats[3 * h + 1 : 3 * h + 2] + stats[3 * h + 2 : 3 * h + 3])
            )
        highest = functools.reduce(jnp.maximum, levels)
        weights = [jnp.exp(level - highest) for level in levels]
        mass = functools.reduce(jnp.add, weights)
        joined = functools.reduce(
            jnp.add,
            [w * part[h * HD : (h + 1) * HD, :].astype(F32) for w, part in zip(weights, parts)],
        )
        attended[:, h * HD : (h + 1) * HD] = jnp.transpose(joined / mass)
    step = keep_ref.shape[0] // blocks
    for block in range(blocks):
        here = pl.ds(pl.multiple_of((2 * block + at[2]) * step, step), step)
        there = pl.ds(pl.multiple_of((2 * block + 1 - at[2]) * step, step), step)
        keep_ref[block * step : (block + 1) * step, :] = attended[here, :].astype(BF16)
        give_ref[block * step : (block + 1) * step, :] = attended[there, :].astype(BF16)


def merge(at, parts, blocks):
    rows = parts[0].shape[1]
    width = parts[0].shape[0] - STAT_ROWS
    half = jax.ShapeDtypeStruct((rows // 2, width), BF16)
    return pl.pallas_call(
        functools.partial(merge_kernel, width // HD, blocks),
        out_shape=(half, half),
        in_specs=[pl.BlockSpec(memory_space=SMEM)]
        + [pl.BlockSpec(memory_space=pltpu.VMEM)] * len(parts),
        out_specs=(pl.BlockSpec(memory_space=pltpu.VMEM),) * 2,
        scratch_shapes=[pltpu.VMEM((rows, width), F32)],
        compiler_params=params(),
        name="merge",
    )(at, *parts)


def output_kernel(count, blocks, at, keep_ref, got_ref, *refs):
    mine, other = refs[:count], refs[count : 2 * count]
    outs, total = refs[2 * count : 2 * count + blocks], refs[2 * count + blocks]
    width = total.shape[1] // (len(mine) // 2) if len(mine) > 1 else total.shape[1]
    depth = keep_ref.shape[1]
    if len(mine) == 1:
        total[...] = jnp.dot(keep_ref[...], mine[0][...], preferred_element_type=F32) + jnp.dot(
            got_ref[...], other[0][...], preferred_element_type=F32
        )
    else:
        half = depth // 2
        groups = [(0,)] + [(2 * k - 1, 2 * k) for k in (1, 2, 3)]
        width = total.shape[1] // 4
        for k, group in enumerate(groups):
            result = 0.0
            for n, index in enumerate(group):
                rows = slice(0, depth) if len(group) == 1 else slice(n * half, (n + 1) * half)
                result = (
                    result
                    + jnp.dot(keep_ref[:, rows], mine[index][...], preferred_element_type=F32)
                    + jnp.dot(got_ref[:, rows], other[index][...], preferred_element_type=F32)
                )
            total[:, k * width : (k + 1) * width] = result
    step = total.shape[0] // blocks
    for k in range(blocks):
        at_row = pl.ds(pl.multiple_of((at[1] ^ k) * step, step), step)
        outs[k][...] = total[at_row, :].astype(BF16)


def output_projection(at, keep, got, mine, other, columns, blocks):
    block = jax.ShapeDtypeStruct((keep.shape[0] // blocks, columns), BF16)
    return pl.pallas_call(
        functools.partial(output_kernel, len(mine), blocks),
        out_shape=(block,) * blocks,
        in_specs=[pl.BlockSpec(memory_space=SMEM)]
        + [pl.BlockSpec(memory_space=pltpu.VMEM)] * (2 + 2 * len(mine)),
        out_specs=(pl.BlockSpec(memory_space=pltpu.VMEM),) * blocks,
        scratch_shapes=[pltpu.VMEM((keep.shape[0], columns), F32)],
        compiler_params=params(),
        cost_estimate=cost(4 * keep.shape[0] * keep.shape[1] * columns, 4 * columns * keep.shape[1]),
        name="output_projection",
    )(at, keep, got, *mine, *other)


def sum_kernel(groups, at, mask_ref, *refs):
    parts, out_ref = refs[:-1], refs[-1]
    width = out_ref.shape[1] // groups
    mask = mask_ref[:, :1]
    for k in range(groups):
        here = slice(k * width, (k + 1) * width)
        total = functools.reduce(jnp.add, [part[:, here].astype(F32) for part in parts])
        total = total * mask
        if groups == 1:
            out_ref[...] = total.astype(BF16)
        else:
            begin = pl.multiple_of((at[0] ^ k) * width, width)
            out_ref[:, pl.ds(begin, width)] = total.astype(BF16)


def final_sum(at, mask, parts, groups):
    return pl.pallas_call(
        functools.partial(sum_kernel, groups),
        out_shape=jax.ShapeDtypeStruct(parts[0].shape, BF16),
        in_specs=[pl.BlockSpec(memory_space=SMEM)]
        + [pl.BlockSpec(memory_space=pltpu.VMEM)] * (1 + len(parts)),
        out_specs=pl.BlockSpec(memory_space=pltpu.VMEM),
        compiler_params=params(),
        name="final_sum",
    )(at, mask, *parts)


def shards(
    hidden_states,
    embeddings,
    norm_gain,
    input_weights,
    adapter_down,
    adapter_up,
    output_weights,
    own_keys,
    own_values,
    shared_keys,
    shared_values,
    cached_lengths,
    prompt_group,
    slot_pages,
    padding_mask,
):
    dp, seq, mp = (lax.axis_index(axis) for axis in ("dp", "seq", "mp"))
    seq_count = lax.axis_size("seq")
    is_end = ((seq == 0) | (seq == seq_count - 1)).astype(jnp.int32)
    at = jnp.stack([dp, seq, mp, is_end, cached_lengths[0], prompt_group[0]])
    pages = slot_pages[0]
    shard = input_weights.shape[0]

    half = norm(at, hidden_states, embeddings, norm_gain[None, :])
    mine = [[half]] + spread(half)
    mine = [[jnp.where(is_end == 1, *slot)] if len(slot) == 2 else slot for slot in mine]
    other = [[lax.ppermute(slot[0], "mp", swap(2, 1))] for slot in mine]

    query_weights = gather_dp(input_weights[:, 0, 0])
    down_0 = gather_down(adapter_down[:, :HD])
    query = project(at, mine, other, query_weights, shard, down_0, adapter_up[0, :, 0])

    key_weights = gather_dp(after(input_weights[:, 1, 0], *last(query_weights)))
    value_weights = gather_dp(after(input_weights[:, 2, 0], *last(key_weights)))
    down_rest = gather_down(after(adapter_down[:, HD:], *last(key_weights)))
    key = project(at, mine, other, key_weights, shard, down_rest[:, :HD], adapter_up[1, :, 0])
    value = project(at, mine, other, value_weights, shard, down_rest[:, HD:], adapter_up[2, :, 0])
    out_own = after(output_weights[0], *last(value_weights))
    if lax.axis_size("dp") == 4:
        out_mine = [piece[0] for piece in gather_dp(out_own)]
    else:
        out_mine = [lax.all_gather(out_own, "dp", axis=1, tiled=True)]
    out_other = [lax.ppermute(piece, "mp", swap(2, 1)) for piece in out_mine]

    slots = [[query]] + spread(query)
    parts = []
    for k, candidates in enumerate(slots):
        part = cache_attention(
            at, pages, k, candidates, own_keys, own_values, shared_keys, shared_values
        )
        parts.append(part if k == 0 else lax.ppermute(part, "seq", swap(seq_count, k)))
    parts.append(new_attention(query, key, value))

    keep, give = merge(at, parts, seq_count)
    got = lax.ppermute(give, "mp", swap(2, 1))
    columns = output_weights.shape[2] * lax.axis_size("dp")
    sums = output_projection(at, keep, got, out_mine, out_other, columns, seq_count)
    sums = [sums[0]] + [lax.ppermute(sums[k], "seq", swap(seq_count, k)) for k in range(1, seq_count)]
    mask = jnp.broadcast_to(padding_mask.astype(F32)[:, None], (padding_mask.shape[0], HD))
    return final_sum(at, mask, sums, 4 if lax.axis_size("dp") == 4 else 1)


def solution(mesh):
    placed = (
        P(("dp", "seq"), None),
        P(("dp", "seq"), None),
        P(),
        P("dp", None, "mp", "seq"),
        P(("seq", "mp"), None),
        P(None, None, "mp", "seq"),
        P("mp", "seq", "dp"),
        P("dp", "seq", "mp"),
        P("dp", "seq", "mp"),
        P(None, "seq", "mp"),
        P(None, "seq", "mp"),
        P("dp"),
        P("dp"),
        P("dp", "seq"),
        P(("dp", "seq", "mp")),
    )
    return jax.shard_map(
        shards, mesh=mesh, in_specs=placed, out_specs=P(("dp", "seq", "mp"), None), check_vma=False
    )
```

```python
import functools
import math

import jax
import jax.numpy as jnp
from jax import lax
from jax.experimental import pallas as pl
from jax.experimental.pallas import tpu as pltpu
from jax.sharding import PartitionSpec as P

HD = 128
PAGE = 64
EPS = 1e-05
NEG = -1e30
STAT_ROWS = 16
MARK = jax.ShapeDtypeStruct((1,), jnp.int32)

SMEM = pltpu.MemorySpace.SMEM
F32 = jnp.float32
BF16 = jnp.bfloat16


def swap(count, k):
    return [(i, i ^ k) for i in range(count)]


def assemble_kernel(plan, *refs):
    out_ref, row = refs[-1], 0
    for index, start, size in plan:
        out_ref[row : row + size, :] = refs[index][start : start + size, :]
        row += size


def assemble(pieces, *earlier):
    arrays = [piece[0] for piece in pieces]
    plan = tuple((n, start, size) for n, (_, start, size) in enumerate(pieces))
    shape = (sum(piece[2] for piece in pieces), arrays[0].shape[1])
    return pl.pallas_call(
        functools.partial(assemble_kernel, plan),
        out_shape=jax.ShapeDtypeStruct(shape, BF16),
        in_specs=[pl.BlockSpec(memory_space=pltpu.VMEM)] * len(arrays)
        + [pl.BlockSpec(memory_space=pl.ANY)] * len(earlier),
        out_specs=pl.BlockSpec(memory_space=pltpu.VMEM),
        compiler_params=params(16),
        cost_estimate=cost(1, 1),
        name="assemble",
    )(*arrays, *earlier)


def cut_kernel(start, *refs):
    out_ref, sem = refs[-2:]
    copy = pltpu.make_async_copy(refs[0].at[start : start + out_ref.shape[0], :], out_ref, sem)
    copy.start()
    copy.wait()


def cut(x, start, size, *earlier):
    return pl.pallas_call(
        functools.partial(cut_kernel, start),
        out_shape=jax.ShapeDtypeStruct((size, x.shape[1]), BF16),
        in_specs=[pl.BlockSpec(memory_space=pl.ANY)] * (1 + len(earlier)),
        out_specs=pl.BlockSpec(memory_space=pltpu.VMEM),
        scratch_shapes=[pltpu.SemaphoreType.DMA(())],
        compiler_params=params(8),
        cost_estimate=cost(1, 1),
        name="cut",
    )(x, *earlier)


def params(mebibytes=16):
    return pltpu.CompilerParams(vmem_limit_bytes=mebibytes * 1024 * 1024)


def cost(flops, moved, transcendentals=0):
    return pl.CostEstimate(flops=1, bytes_accessed=1, transcendentals=0)


def spread(x):
    count = lax.axis_size("seq")
    blocks = {0: x}
    for k in sorted(range(1, count), key=lambda k: k.bit_count()):
        step = k & -k
        blocks[k] = lax.ppermute(blocks[k ^ step], "seq", swap(count, step))
    return [blocks[k] for k in range(count)]


def along_x(x):
    return lax.ppermute(x, "dp", swap(4, 1))


def along_y(x):
    return lax.ppermute(x, "dp", swap(4, 2))


def both_ways(x):
    return along_x(x), along_y(x)


def halves_on(by_x, by_y, small, *gate):
    half = by_x.shape[0] // 2
    rest = [] if small is None else [(small, 0, small.shape[0])]
    top = along_y(assemble([(by_x, 0, half)] + rest, *gate))
    bottom = along_x(assemble([(by_y, half, half)] + rest, *gate))
    return top, bottom


def other_core(x):
    return lax.ppermute(x, "mp", swap(2, 1))


def norm_kernel(down_rows, at, *refs):
    count = (len(refs) - 3) // 2
    sources, (out_ref, mark), held, sems = (
        refs[:count],
        refs[count : count + 2],
        refs[count + 2 : -1],
        refs[-1],
    )
    mark[0] = jnp.int32(0)
    copies = [
        pltpu.make_async_copy(source, target, sems.at[n])
        for n, (source, target) in enumerate(zip(sources, held))
    ]
    for copy in copies:
        copy.start()
    for copy in copies:
        copy.wait()
    hidden_ref, embed_ref, gain_ref = held[:3]
    hidden = hidden_ref[...].astype(F32)
    embed = embed_ref[...].astype(F32)
    rows, width = hidden.shape
    squares = jnp.sum(hidden * hidden, axis=1, keepdims=True) + jnp.sum(
        embed * embed, axis=1, keepdims=True
    )
    factor = lax.rsqrt(squares / (2 * width) + EPS)

    @pl.when(at[2] == 0)
    def _():
        out_ref[:rows, :] = (hidden * factor * gain_ref[:, :width]).astype(BF16)

    @pl.when(at[2] != 0)
    def _():
        out_ref[:rows, :] = (embed * factor * gain_ref[:, width:]).astype(BF16)

    if down_rows is not None:
        whole = jnp.transpose(held[3][:, :HD].astype(F32)).astype(BF16)
        own = pl.ds(pl.multiple_of(at[0] * down_rows, down_rows), down_rows)
        part = jnp.transpose(held[3][own, HD:].astype(F32)).astype(BF16)
        for x in (whole, part):
            groups = width // x.shape[1]
            step = x.shape[0] // groups
            for g in range(groups):
                columns = slice(g * x.shape[1], (g + 1) * x.shape[1])
                out_ref[rows : rows + step, columns] = x[g * step : (g + 1) * step, :]
            rows += step


def norm(at, hidden, embed, gain, down, down_rows):
    rows, width = hidden.shape
    arrays = (hidden, embed, gain)
    if down_rows is not None:
        arrays += (down,)
        rows += HD * down.shape[0] // width + 2 * HD * down_rows // width
    return pl.pallas_call(
        functools.partial(norm_kernel, down_rows),
        out_shape=(jax.ShapeDtypeStruct((rows, width), BF16), MARK),
        in_specs=[pl.BlockSpec(memory_space=SMEM)]
        + [pl.BlockSpec(memory_space=pl.ANY)] * len(arrays),
        out_specs=(pl.BlockSpec(memory_space=pltpu.VMEM), pl.BlockSpec(memory_space=SMEM)),
        scratch_shapes=[pltpu.VMEM(x.shape, x.dtype) for x in arrays]
        + [pltpu.SemaphoreType.DMA((len(arrays),))],
        compiler_params=params(60),
        cost_estimate=cost(1, 1),
        name="norm",
    )(at, *arrays)


def arrange_kernel(begin, *refs):
    count = len(refs) - 4
    sources, out_ref, held, sems = refs[:count], refs[-3], refs[-2], refs[-1]
    step, width = held.shape[1:]
    copies = [
        pltpu.make_async_copy(source.at[begin : begin + step, :], held.at[n], sems.at[n])
        for n, source in enumerate(sources)
    ]
    for copy in copies:
        copy.start()
    for copy in copies:
        copy.wait()
    size = out_ref.shape[1] // count
    for n in range(count):
        for g in range(width // size):
            out_ref[g * step : (g + 1) * step, n * size : (n + 1) * size] = held[
                n, :, g * size : (g + 1) * size
            ]


def arrange(blocks, earlier, begin, down_rows):
    width = blocks[0].shape[1]
    step = 2 * HD * down_rows // width
    return pl.pallas_call(
        functools.partial(arrange_kernel, begin),
        out_shape=jax.ShapeDtypeStruct((2 * HD, len(blocks) * down_rows), BF16),
        in_specs=[pl.BlockSpec(memory_space=pl.ANY)] * (len(blocks) + 1),
        out_specs=pl.BlockSpec(memory_space=pltpu.VMEM),
        scratch_shapes=[
            pltpu.VMEM((len(blocks), step, width), BF16),
            pltpu.SemaphoreType.DMA((len(blocks),)),
        ],
        cost_estimate=cost(1, 1),
        name="arrange",
    )(*blocks, earlier)


def project_kernel(plan, at, *refs):
    slots, count, inputs, down_rows = plan
    arrays, outs = refs[:count], refs[count : count + len(inputs)]
    mark, joined, down = refs[count + len(inputs) :]
    mark[0] = jnp.int32(0)
    dp, seq, core = at[0], at[1], at[2]
    rows = joined.shape[0] // len(slots)
    width = joined.shape[1] // 2

    def part(begin, size):
        return pl.ds(pl.multiple_of(begin, size), size)

    for k, (mine, other) in enumerate(slots):
        at_row = part((seq ^ k) * rows, rows)
        joined[at_row, part(core * width, width)] = arrays[mine][:rows, :]
        joined[at_row, part((1 - core) * width, width)] = arrays[other][:rows, :]
    for n, (_, downs, _) in enumerate(inputs):
        if down_rows is None:
            down[:, n * HD : (n + 1) * HD] = arrays[downs][...]
            continue
        if downs is None:
            size = (joined.shape[1] // 2) // len(slots)
            step = HD * size // width
            for k, pair in enumerate(slots):
                for crossed, index in enumerate(pair):
                    columns = part(((seq ^ k) * 2 + (core ^ crossed)) * size, size)
                    for g in range(width // size):
                        down[g * step : (g + 1) * step, columns] = arrays[index][
                            rows : rows + step, g * size : (g + 1) * size
                        ]
            continue
        for index, row, k, crossed in downs:
            for j in range(4):
                begin = (((seq ^ j) * 2 + (core ^ crossed)) * 4 + (dp ^ k)) * down_rows
                down[n * HD : (n + 1) * HD, part(begin, down_rows)] = arrays[index][
                    row : row + HD, j * down_rows : (j + 1) * down_rows
                ]
    if down_rows is None:
        low = jnp.dot(joined[...], down[...], preferred_element_type=F32).astype(BF16)
    else:
        low = scores_of(joined[...], down[...]).astype(BF16)
    for n, ((weights, _, up), out) in enumerate(zip(inputs, outs)):
        total = jnp.dot(
            low[:, n * HD : (n + 1) * HD], arrays[up][...], preferred_element_type=F32
        )
        for index, row, size, k, start, shard in weights:
            columns = joined[...] if k is None else joined[:, part((dp ^ k) * shard + start, size)]
            total += jnp.dot(columns, arrays[index][row : row + size, :], preferred_element_type=F32)
        out[...] = total.astype(BF16)


def project(at, slots, rows, inputs, down_rows):
    arrays = []

    def place(array):
        for index, known in enumerate(arrays):
            if known is array:
                return index
        arrays.append(array)
        return len(arrays) - 1

    placed = tuple(tuple(place(x) for x in slot) for slot in slots)
    plans = []
    for weights, downs, up in inputs:
        weights = tuple((place(piece[0]), *piece[1:]) for piece in weights)
        if down_rows is None:
            downs = place(downs)
        elif downs is not None:
            downs = tuple((place(piece[0]), *piece[1:]) for piece in downs)
        plans.append((weights, downs, place(up)))
    width = 2 * slots[0][0].shape[1]
    columns = inputs[0][2].shape[1]
    result = jax.ShapeDtypeStruct((rows, columns), BF16)
    ranks = len(inputs) * HD
    return pl.pallas_call(
        functools.partial(project_kernel, (placed, len(arrays), tuple(plans), down_rows)),
        out_shape=(*(result,) * len(inputs), MARK),
        in_specs=[pl.BlockSpec(memory_space=SMEM)]
        + [pl.BlockSpec(memory_space=pltpu.VMEM)] * len(arrays),
        out_specs=(
            *(pl.BlockSpec(memory_space=pltpu.VMEM),) * len(inputs),
            pl.BlockSpec(memory_space=SMEM),
        ),
        scratch_shapes=[
            pltpu.VMEM((rows, width), BF16),
            pltpu.VMEM((width, ranks) if down_rows is None else (ranks, width), BF16),
        ],
        compiler_params=params((20 if len(inputs) == 1 else 32) if down_rows is not None else 40),
        cost_estimate=cost(
            2 * rows * width * (columns + HD) * len(inputs), 2 * width * (rows + columns * len(inputs))
        ),
        name="project",
    )(at, *arrays)


def finish_head(head, heads, weighted, peak, total, out_ref, stats):
    level = peak + jnp.log(total)
    high = level.astype(BF16).astype(F32)
    rest = level - high
    mid = rest.astype(BF16).astype(F32)
    stats[3 * head : 3 * head + 1, :] = high
    stats[3 * head + 1 : 3 * head + 2, :] = mid
    stats[3 * head + 2 : 3 * head + 3, :] = rest - mid
    out_ref[head * HD : (head + 1) * HD, :] = (weighted / total).astype(BF16)
    if head == heads - 1:
        out_ref[heads * HD :, :] = stats[...].astype(BF16)


def over_keys(left, right):
    return lax.dot_general(left, right, (((0,), (0,)), ((), ())), preferred_element_type=F32)


def scores_of(keys, queries):
    return lax.dot_general(keys, queries, (((1,), (1,)), ((), ())), preferred_element_type=F32)


def cache_kernel(
    slot,
    heads,
    at,
    earlier,
    pages,
    query_ref,
    key_ref,
    value_ref,
    shared_key_ref,
    shared_value_ref,
    out_ref,
    mark,
    stats,
):
    mark[0] = jnp.int32(0)
    stats[...] = jnp.zeros_like(stats)
    scale = 1.0 / math.sqrt(HD)
    group = at[4]
    for head in range(heads):
        columns = pl.ds(pl.multiple_of(((at[1] ^ slot) * heads + head) * HD, HD), HD)
        queries = query_ref[:, head * HD : (head + 1) * HD]
        own = scores_of(key_ref[0, :, columns], queries) * scale
        shared = scores_of(shared_key_ref[group, :, columns], queries) * scale
        offset = lax.broadcasted_iota(jnp.int32, (PAGE, own.shape[1]), 0)
        masked = []
        for u in range(own.shape[0] // PAGE):
            usable = offset < at[3] - pages[u] * PAGE
            masked.append(jnp.where(usable, own[u * PAGE : (u + 1) * PAGE], NEG))
        own = jnp.concatenate(masked, axis=0)
        peak = jnp.maximum(
            jnp.max(own, axis=0, keepdims=True), jnp.max(shared, axis=0, keepdims=True)
        )
        own = jnp.exp(own - peak)
        shared = jnp.exp(shared - peak)
        total = jnp.sum(own, axis=0, keepdims=True) + jnp.sum(shared, axis=0, keepdims=True)
        weighted = over_keys(value_ref[0, :, columns], own.astype(BF16)) + over_keys(
            shared_value_ref[group, :, columns], shared.astype(BF16)
        )
        finish_head(head, heads, weighted, peak, total, out_ref, stats)


def cache_attention(at, earlier, pages, slot, queries, own_keys, own_values, shared_keys, shared_values):
    rows, width = queries.shape
    heads = width // HD
    slots, shared_slots = own_keys.shape[1], shared_keys.shape[1]
    return pl.pallas_call(
        functools.partial(cache_kernel, slot, heads),
        out_shape=(jax.ShapeDtypeStruct((width + STAT_ROWS, rows), BF16), MARK),
        in_specs=[pl.BlockSpec(memory_space=SMEM)] * 3
        + [pl.BlockSpec(memory_space=pltpu.VMEM)] * 5,
        out_specs=(pl.BlockSpec(memory_space=pltpu.VMEM), pl.BlockSpec(memory_space=SMEM)),
        scratch_shapes=[pltpu.VMEM((STAT_ROWS, rows), F32)],
        compiler_params=params(16),
        cost_estimate=cost(
            8 * rows * width * (slots + shared_slots),
            4 * width * (slots + shared_slots),
            rows * heads * (slots + shared_slots),
        ),
        name="cache_attention",
    )(at, earlier, pages, queries, own_keys, own_values, shared_keys, shared_values)


def new_kernel(heads, query_ref, key_ref, value_ref, out_ref, stats):
    stats[...] = jnp.zeros_like(stats)
    for head in range(heads):
        columns = slice(head * HD, (head + 1) * HD)
        scores = scores_of(key_ref[:, columns], query_ref[:, columns]) * (1.0 / math.sqrt(HD))
        places = lax.broadcasted_iota(jnp.int32, scores.shape, 0)
        tokens = lax.broadcasted_iota(jnp.int32, scores.shape, 1)
        scores = jnp.where(places <= tokens, scores, NEG)
        peak = jnp.max(scores, axis=0, keepdims=True)
        exponent = jnp.exp(scores - peak)
        total = jnp.sum(exponent, axis=0, keepdims=True)
        weighted = over_keys(value_ref[:, columns], exponent.astype(BF16))
        finish_head(head, heads, weighted, peak, total, out_ref, stats)


def new_attention(queries, keys, values):
    rows, width = queries.shape
    heads = width // HD
    return pl.pallas_call(
        functools.partial(new_kernel, heads),
        out_shape=jax.ShapeDtypeStruct((width + STAT_ROWS, rows), BF16),
        in_specs=[pl.BlockSpec(memory_space=pltpu.VMEM)] * 3,
        out_specs=pl.BlockSpec(memory_space=pltpu.VMEM),
        scratch_shapes=[pltpu.VMEM((STAT_ROWS, rows), F32)],
        compiler_params=params(16),
        cost_estimate=cost(8 * rows * rows * width, 8 * rows * width, rows * rows * heads),
        name="new_attention",
    )(queries, keys, values)


def merge_kernel(heads, blocks, at, *refs):
    parts = refs[: len(refs) - 3]
    keep_ref, give_ref, attended = refs[len(refs) - 3 :]
    base = heads * HD
    for h in range(heads):
        levels = []
        for part in parts:
            stats = part[base : base + STAT_ROWS, :].astype(F32)
            levels.append(
                stats[3 * h : 3 * h + 1] + (stats[3 * h + 1 : 3 * h + 2] + stats[3 * h + 2 : 3 * h + 3])
            )
        highest = functools.reduce(jnp.maximum, levels)
        weights = [jnp.exp(level - highest) for level in levels]
        mass = functools.reduce(jnp.add, weights)
        joined = functools.reduce(
            jnp.add,
            [w * part[h * HD : (h + 1) * HD, :].astype(F32) for w, part in zip(weights, parts)],
        )
        attended[:, h * HD : (h + 1) * HD] = jnp.transpose(joined / mass)
    step = keep_ref.shape[0] // blocks
    for block in range(blocks):
        here = pl.ds(pl.multiple_of((2 * block + at[2]) * step, step), step)
        there = pl.ds(pl.multiple_of((2 * block + 1 - at[2]) * step, step), step)
        keep_ref[block * step : (block + 1) * step, :] = attended[here, :].astype(BF16)
        give_ref[block * step : (block + 1) * step, :] = attended[there, :].astype(BF16)


def merge(at, parts, blocks):
    rows = parts[0].shape[1]
    width = parts[0].shape[0] - STAT_ROWS
    half = jax.ShapeDtypeStruct((rows // 2, width), BF16)
    return pl.pallas_call(
        functools.partial(merge_kernel, width // HD, blocks),
        out_shape=(half, half),
        in_specs=[pl.BlockSpec(memory_space=SMEM)]
        + [pl.BlockSpec(memory_space=pltpu.VMEM)] * len(parts),
        out_specs=(pl.BlockSpec(memory_space=pltpu.VMEM),) * 2,
        scratch_shapes=[pltpu.VMEM((rows, width), F32)],
        compiler_params=params(),
        cost_estimate=cost(1, 1),
        name="merge",
    )(at, *parts)


def output_kernel(count, blocks, at, keep_ref, got_ref, *refs):
    mine, other = refs[:count], refs[count : len(refs) - blocks - 1]
    outs, total = refs[-1 - blocks : -1], refs[-1]
    depth = keep_ref.shape[1]
    groups = 4 if count == 5 else 1
    width = total.shape[1] // groups
    for k in range(groups):
        if k < 3:
            here = jnp.dot(keep_ref[...], mine[k][...], preferred_element_type=F32)
            there = other[0][k * depth : (k + 1) * depth, :]
        else:
            half = depth // 2
            here = jnp.dot(keep_ref[:, :half], mine[3][...], preferred_element_type=F32)
            here += jnp.dot(keep_ref[:, half:], mine[4][...], preferred_element_type=F32)
            there = other[1][...]
        here += jnp.dot(got_ref[...], there, preferred_element_type=F32)
        total[:, k * width : (k + 1) * width] = here
    step = total.shape[0] // blocks
    for k in range(blocks):
        at_row = pl.ds(pl.multiple_of((at[1] ^ k) * step, step), step)
        outs[k][...] = total[at_row, :].astype(BF16)


def output_projection(at, keep, got, mine, other, blocks):
    columns = mine[0].shape[1] * (4 if len(mine) == 5 else 1)
    block = jax.ShapeDtypeStruct((keep.shape[0] // blocks, columns), BF16)
    return pl.pallas_call(
        functools.partial(output_kernel, len(mine), blocks),
        out_shape=(block,) * blocks,
        in_specs=[pl.BlockSpec(memory_space=SMEM)]
        + [pl.BlockSpec(memory_space=pltpu.VMEM)] * (2 + len(mine) + len(other)),
        out_specs=(pl.BlockSpec(memory_space=pltpu.VMEM),) * blocks,
        scratch_shapes=[pltpu.VMEM((keep.shape[0], columns), F32)],
        compiler_params=params(20),
        cost_estimate=cost(1, 1),
        name="output_projection",
    )(at, keep, got, *mine, *other)


def sum_kernel(groups, at, mask_ref, *refs):
    parts, out_ref = refs[:-1], refs[-1]
    width = out_ref.shape[1] // groups
    mask = mask_ref[:, :1]
    for k in range(groups):
        here = slice(k * width, (k + 1) * width)
        total = functools.reduce(jnp.add, [part[:, here].astype(F32) for part in parts])
        total = total * mask
        if groups == 1:
            out_ref[...] = total.astype(BF16)
        else:
            begin = pl.multiple_of((at[0] ^ k) * width, width)
            out_ref[:, pl.ds(begin, width)] = total.astype(BF16)


def final_sum(at, mask, parts, groups):
    return pl.pallas_call(
        functools.partial(sum_kernel, groups),
        out_shape=jax.ShapeDtypeStruct(parts[0].shape, BF16),
        in_specs=[pl.BlockSpec(memory_space=SMEM)]
        + [pl.BlockSpec(memory_space=pltpu.VMEM)] * (1 + len(parts)),
        out_specs=pl.BlockSpec(memory_space=pltpu.VMEM),
        compiler_params=params(),
        cost_estimate=cost(1, 1),
        name="final_sum",
    )(at, mask, *parts)


def query_4(at, blocks, rows, weights, up, down_rows, *gate):
    shard = weights.shape[0]
    half = shard // 2
    by_x, by_y = both_ways(weights)
    top, bottom = halves_on(by_x, by_y, None, *gate)
    pieces = [(x, 0, shard, k, 0, shard) for k, x in enumerate((weights, by_x, by_y))]
    pieces += [(top, 0, half, 3, 0, shard), (bottom, 0, half, 3, half, shard)]
    query, mark = project(at, blocks, rows, [(pieces, None, up)], down_rows)
    return query, mark, [top, bottom]


def key_value_4(at, blocks, rows, weights, near, last, downs, ups, down_rows, *late):
    shard = weights.shape[0] // 2
    other = other_core(assemble([(x, row, 2 * HD) for x, row in downs], *late))
    inputs = []
    for n in range(2):
        pieces = [(x, n * shard, shard, k, 0, shard) for k, x in enumerate((weights, *near))]
        pieces.append((last[n], 0, shard, 3, 0, shard))
        small = [(x, row + n * HD, k, 0) for k, (x, row) in enumerate(downs)]
        small += [(other, (2 * k + n) * HD, k, 1) for k in range(4)]
        inputs.append((pieces, small, ups[n]))
    return project(at, blocks, rows, inputs, down_rows)


def shards(
    hidden_states,
    embeddings,
    norm_gain,
    input_weights,
    adapter_down,
    adapter_up,
    output_weights,
    own_keys,
    own_values,
    shared_keys,
    shared_values,
    cached_lengths,
    prompt_group,
    slot_pages,
    padding_mask,
):
    dp, seq, mp = (lax.axis_index(axis) for axis in ("dp", "seq", "mp"))
    seq_count = lax.axis_size("seq")
    by_four = lax.axis_size("dp") == 4 and seq_count == 4
    at = jnp.stack([dp, seq, mp, cached_lengths[0], prompt_group[0]])
    pages = slot_pages[0]
    ups = [adapter_up[p, :, 0] for p in range(3)]
    down_rows = adapter_down.shape[0] // 4

    own_rows = hidden_states.shape[0]
    rows = own_rows * seq_count
    half, mark = norm(
        at,
        hidden_states,
        embeddings,
        norm_gain[None, :],
        adapter_down,
        down_rows if by_four else None,
    )
    mine = spread(half)
    blocks = [(block, other_core(block)) for block in mine]
    shard, _, _, width = input_weights.shape
    if by_four:
        own_weights = jnp.transpose(input_weights[:, :, 0], (1, 0, 2)).reshape(-1, width)
        weights = cut(own_weights, 0, shard, mark)
        query, mark, arrived = query_4(at, blocks, rows, weights, ups[0], down_rows, mine[2])
    else:
        whole = lax.all_gather(input_weights[:, :, 0], "dp", axis=0, tiled=True)
        down = lax.all_gather(adapter_down, ("seq", "mp"), axis=0, tiled=True)
        inputs = [
            ([(whole[:, p], 0, whole.shape[0], None, 0, 0)], down[:, p * HD : (p + 1) * HD], ups[p])
            for p in range(3)
        ]
        query, key, value, mark = project(at, blocks, rows, inputs, None)
    queries = spread(query)

    parts, sent, marks = {}, {}, [mark]
    for k in range(seq_count):
        parts[k], mark = cache_attention(
            at,
            marks[-1],
            pages,
            k,
            queries[k],
            own_keys,
            own_values,
            shared_keys,
            shared_values,
        )
        marks.append(mark)
        sent[k] = lax.ppermute(parts[k], "seq", swap(seq_count, k)) if k else parts[k]

    if by_four:
        begin = own_rows + HD * adapter_down.shape[0] // half.shape[1]
        down = arrange(mine, marks[0], begin, down_rows)
        exchanged = [block[1] for block in blocks[:3]]
        weights = cut(own_weights, shard, 2 * shard, mine[3], *exchanged, *arrived)
        near = both_ways(weights)
        far = lax.ppermute(down, "dp", swap(4, 3))
        output_own = cut(output_weights[0], 0, output_weights.shape[1], *near, far, marks[3])
        by_x, by_y = both_ways(output_own)
        last = halves_on(*near, down, by_x, by_y, queries[3])
        top, bottom = halves_on(by_x, by_y, None, *last)
        downs = [(down, 0), (last[1], shard), (last[0], shard), (far, 0)]
        key, value, _ = key_value_4(
            at, blocks, rows, weights, near, last, downs, ups[1:], down_rows, *list(sent.values())[1:]
        )
        out_mine = [output_own, by_x, by_y, top, bottom]
        out_other = [
            other_core(assemble([(x, 0, x.shape[0]) for x in part]))
            for part in (out_mine[:3], out_mine[3:])
        ]
    else:
        out_mine = [lax.all_gather(output_weights[0], "dp", axis=1, tiled=True)]
        out_other = [other_core(out_mine[0])]

    joined = [sent[k] for k in range(seq_count)] + [new_attention(query, key, value)]
    keep, give = merge(at, joined, seq_count)
    got = other_core(give)
    sums = output_projection(at, keep, got, out_mine, out_other, seq_count)
    sums = [sums[0]] + [lax.ppermute(sums[k], "seq", swap(seq_count, k)) for k in range(1, seq_count)]
    mask = jnp.broadcast_to(padding_mask.astype(F32)[:, None], (padding_mask.shape[0], HD))
    return final_sum(at, mask, sums, 4 if by_four else 1)


def solution(mesh):
    placed = (
        P(("dp", "seq"), None),
        P(("dp", "seq"), None),
        P(),
        P("dp", None, "mp", "seq"),
        P(("seq", "mp"), None),
        P(None, None, "mp", "seq"),
        P("mp", "seq", "dp"),
        P("dp", "seq", "mp"),
        P("dp", "seq", "mp"),
        P(None, "seq", "mp"),
        P(None, "seq", "mp"),
        P("dp"),
        P("dp"),
        P("dp", "seq"),
        P(("dp", "seq", "mp")),
    )
    return jax.shard_map(
        shards, mesh=mesh, in_specs=placed, out_specs=P(("dp", "seq", "mp"), None), check_vma=False
    )
```

```python
import functools
import math

import jax
import jax.numpy as jnp
from jax import lax
from jax.experimental import pallas as pl
from jax.experimental.pallas import tpu as pltpu
from jax.sharding import PartitionSpec as P

HD = 128
PAGE = 64
EPS = 1e-05
NEG = -1e30
STAT_ROWS = 16
MARK = jax.ShapeDtypeStruct((1,), jnp.int32)

SMEM = pltpu.MemorySpace.SMEM
F32 = jnp.float32
BF16 = jnp.bfloat16


def swap(count, k):
    return [(i, i ^ k) for i in range(count)]


def assemble_kernel(plan, *refs):
    out_ref, row = refs[-1], 0
    for index, start, size in plan:
        out_ref[row : row + size, :] = refs[index][start : start + size, :]
        row += size


def assemble(pieces, *earlier):
    arrays = [piece[0] for piece in pieces]
    plan = tuple((n, start, size) for n, (_, start, size) in enumerate(pieces))
    shape = (sum(piece[2] for piece in pieces), arrays[0].shape[1])
    return pl.pallas_call(
        functools.partial(assemble_kernel, plan),
        out_shape=jax.ShapeDtypeStruct(shape, BF16),
        in_specs=[pl.BlockSpec(memory_space=pltpu.VMEM)] * len(arrays)
        + [pl.BlockSpec(memory_space=pl.ANY)] * len(earlier),
        out_specs=pl.BlockSpec(memory_space=pltpu.VMEM),
        compiler_params=params(16),
        cost_estimate=cost(1, 1),
        name="assemble",
    )(*arrays, *earlier)


def cut_kernel(start, *refs):
    out_ref, sem = refs[-2:]
    copy = pltpu.make_async_copy(refs[0].at[start : start + out_ref.shape[0], :], out_ref, sem)
    copy.start()
    copy.wait()


def cut(x, start, size, *earlier):
    return pl.pallas_call(
        functools.partial(cut_kernel, start),
        out_shape=jax.ShapeDtypeStruct((size, x.shape[1]), BF16),
        in_specs=[pl.BlockSpec(memory_space=pl.ANY)] * (1 + len(earlier)),
        out_specs=pl.BlockSpec(memory_space=pltpu.VMEM),
        scratch_shapes=[pltpu.SemaphoreType.DMA(())],
        compiler_params=params(8),
        cost_estimate=cost(1, 1),
        name="cut",
    )(x, *earlier)


def params(mebibytes=16):
    return pltpu.CompilerParams(vmem_limit_bytes=mebibytes * 1024 * 1024)


def cost(flops, moved, transcendentals=0):
    return pl.CostEstimate(flops=1, bytes_accessed=1, transcendentals=0)


def spread(x):
    count = lax.axis_size("seq")
    blocks = {0: x}
    for k in sorted(range(1, count), key=lambda k: k.bit_count()):
        step = k & -k
        blocks[k] = lax.ppermute(blocks[k ^ step], "seq", swap(count, step))
    return [blocks[k] for k in range(count)]


def along_x(x):
    return lax.ppermute(x, "dp", swap(4, 1))


def along_y(x):
    return lax.ppermute(x, "dp", swap(4, 2))


def both_ways(x):
    return along_x(x), along_y(x)


def halves_on(by_x, by_y, small, *gate):
    half = by_x.shape[0] // 2
    rest = [] if small is None else [(small, 0, small.shape[0])]
    top = along_y(assemble([(by_x, 0, half)] + rest, *gate))
    bottom = along_x(assemble([(by_y, half, half)] + rest, *gate))
    return top, bottom


def other_core(x):
    return lax.ppermute(x, "mp", swap(2, 1))


def norm_kernel(down_rows, at, *refs):
    count = (len(refs) - 3) // 2
    sources, (out_ref, mark), held, sems = (
        refs[:count],
        refs[count : count + 2],
        refs[count + 2 : -1],
        refs[-1],
    )
    mark[0] = jnp.int32(0)
    copies = [
        pltpu.make_async_copy(source, target, sems.at[n])
        for n, (source, target) in enumerate(zip(sources, held))
    ]
    for copy in copies:
        copy.start()
    for copy in copies:
        copy.wait()
    hidden_ref, embed_ref, gain_ref = held[:3]
    hidden = hidden_ref[...].astype(F32)
    embed = embed_ref[...].astype(F32)
    rows, width = hidden.shape
    squares = jnp.sum(hidden * hidden, axis=1, keepdims=True) + jnp.sum(
        embed * embed, axis=1, keepdims=True
    )
    factor = lax.rsqrt(squares / (2 * width) + EPS)

    @pl.when(at[2] == 0)
    def _():
        out_ref[:rows, :] = (hidden * factor * gain_ref[:, :width]).astype(BF16)

    @pl.when(at[2] != 0)
    def _():
        out_ref[:rows, :] = (embed * factor * gain_ref[:, width:]).astype(BF16)

    if down_rows is not None:
        whole = jnp.transpose(held[3][:, :HD].astype(F32)).astype(BF16)
        own = pl.ds(pl.multiple_of(at[0] * down_rows, down_rows), down_rows)
        part = jnp.transpose(held[3][own, HD:].astype(F32)).astype(BF16)
        for x in (whole, part):
            groups = width // x.shape[1]
            step = x.shape[0] // groups
            for g in range(groups):
                columns = slice(g * x.shape[1], (g + 1) * x.shape[1])
                out_ref[rows : rows + step, columns] = x[g * step : (g + 1) * step, :]
            rows += step


def norm(at, hidden, embed, gain, down, down_rows):
    rows, width = hidden.shape
    arrays = (hidden, embed, gain)
    if down_rows is not None:
        arrays += (down,)
        rows += HD * down.shape[0] // width + 2 * HD * down_rows // width
    return pl.pallas_call(
        functools.partial(norm_kernel, down_rows),
        out_shape=(jax.ShapeDtypeStruct((rows, width), BF16), MARK),
        in_specs=[pl.BlockSpec(memory_space=SMEM)]
        + [pl.BlockSpec(memory_space=pl.ANY)] * len(arrays),
        out_specs=(pl.BlockSpec(memory_space=pltpu.VMEM), pl.BlockSpec(memory_space=SMEM)),
        scratch_shapes=[pltpu.VMEM(x.shape, x.dtype) for x in arrays]
        + [pltpu.SemaphoreType.DMA((len(arrays),))],
        compiler_params=params(60),
        cost_estimate=cost(1, 1),
        name="norm",
    )(at, *arrays)


def arrange_kernel(begin, *refs):
    count = len(refs) - 4
    sources, out_ref, held, sems = refs[:count], refs[-3], refs[-2], refs[-1]
    step, width = held.shape[1:]
    copies = [
        pltpu.make_async_copy(source.at[begin : begin + step, :], held.at[n], sems.at[n])
        for n, source in enumerate(sources)
    ]
    for copy in copies:
        copy.start()
    for copy in copies:
        copy.wait()
    size = out_ref.shape[1] // count
    for n in range(count):
        for g in range(width // size):
            out_ref[g * step : (g + 1) * step, n * size : (n + 1) * size] = held[
                n, :, g * size : (g + 1) * size
            ]


def arrange(blocks, earlier, begin, down_rows):
    width = blocks[0].shape[1]
    step = 2 * HD * down_rows // width
    return pl.pallas_call(
        functools.partial(arrange_kernel, begin),
        out_shape=jax.ShapeDtypeStruct((2 * HD, len(blocks) * down_rows), BF16),
        in_specs=[pl.BlockSpec(memory_space=pl.ANY)] * (len(blocks) + 1),
        out_specs=pl.BlockSpec(memory_space=pltpu.VMEM),
        scratch_shapes=[
            pltpu.VMEM((len(blocks), step, width), BF16),
            pltpu.SemaphoreType.DMA((len(blocks),)),
        ],
        cost_estimate=cost(1, 1),
        name="arrange",
    )(*blocks, earlier)


def project_kernel(plan, stage, at, *refs):
    slots, count, inputs, down_rows = plan
    arrays, outs = refs[:count], refs[count : count + len(inputs)]
    mark, joined, down = refs[count + len(inputs) :]
    mark[0] = jnp.int32(0)
    dp, seq, core = at[0], at[1], at[2]
    rows = joined.shape[0] // len(slots)
    width = joined.shape[1] // 2

    def part(begin, size):
        return pl.ds(pl.multiple_of(begin, size), size)

    for k, (mine, other) in enumerate(slots):
        at_row = part((seq ^ k) * rows, rows)
        joined[at_row, part(core * width, width)] = arrays[mine][:rows, :]
        joined[at_row, part((1 - core) * width, width)] = arrays[other][:rows, :]
    for n, (_, downs, _, _) in enumerate(inputs if stage != 1 else ()):
        if down_rows is None:
            down[:, n * HD : (n + 1) * HD] = arrays[downs][...]
            continue
        if downs is None:
            size = (joined.shape[1] // 2) // len(slots)
            step = HD * size // width
            for k, pair in enumerate(slots):
                for crossed, index in enumerate(pair):
                    columns = part(((seq ^ k) * 2 + (core ^ crossed)) * size, size)
                    for g in range(width // size):
                        down[g * step : (g + 1) * step, columns] = arrays[index][
                            rows : rows + step, g * size : (g + 1) * size
                        ]
            continue
        for index, row, k, crossed in downs:
            for j in range(4):
                begin = (((seq ^ j) * 2 + (core ^ crossed)) * 4 + (dp ^ k)) * down_rows
                down[n * HD : (n + 1) * HD, part(begin, down_rows)] = arrays[index][
                    row : row + HD, j * down_rows : (j + 1) * down_rows
                ]
    if stage == 1:
        low = None
    elif down_rows is None:
        low = jnp.dot(joined[...], down[...], preferred_element_type=F32).astype(BF16)
    else:
        low = scores_of(joined[...], down[...]).astype(BF16)
    for n, ((weights, _, up, begun), out) in enumerate(zip(inputs, outs)):
        total = 0.0
        if stage != 1:
            total = jnp.dot(
                low[:, n * HD : (n + 1) * HD], arrays[up][...], preferred_element_type=F32
            )
        if begun is not None:
            total += arrays[begun][...]
        for index, row, size, k, start, shard in weights:
            columns = joined[...] if k is None else joined[:, part((dp ^ k) * shard + start, size)]
            total += jnp.dot(columns, arrays[index][row : row + size, :], preferred_element_type=F32)
        out[...] = total.astype(out.dtype)


def project(at, slots, rows, inputs, down_rows, stage=0, begun=(None, None, None)):
    arrays = []

    def place(array):
        for index, known in enumerate(arrays):
            if known is array:
                return index
        arrays.append(array)
        return len(arrays) - 1

    placed = tuple(tuple(place(x) for x in slot) for slot in slots)
    plans = []
    for (weights, downs, up), so_far in zip(inputs, begun):
        weights = tuple((place(piece[0]), *piece[1:]) for piece in weights)
        if stage == 1:
            downs = None
        elif down_rows is None:
            downs = place(downs)
        elif downs is not None:
            downs = tuple((place(piece[0]), *piece[1:]) for piece in downs)
        so_far = None if so_far is None else place(so_far)
        plans.append((weights, downs, None if stage == 1 else place(up), so_far))
    width = 2 * slots[0][0].shape[1]
    columns = inputs[0][2].shape[1]
    result = jax.ShapeDtypeStruct((rows, columns), F32 if stage == 1 else BF16)
    ranks = len(inputs) * HD
    return pl.pallas_call(
        functools.partial(project_kernel, (placed, len(arrays), tuple(plans), down_rows), stage),
        out_shape=(*(result,) * len(inputs), MARK),
        in_specs=[pl.BlockSpec(memory_space=SMEM)]
        + [pl.BlockSpec(memory_space=pltpu.VMEM)] * len(arrays),
        out_specs=(
            *(pl.BlockSpec(memory_space=pltpu.VMEM),) * len(inputs),
            pl.BlockSpec(memory_space=SMEM),
        ),
        scratch_shapes=[
            pltpu.VMEM((rows, width), BF16),
            pltpu.VMEM((width, ranks) if down_rows is None else (ranks, width), BF16),
        ],
        compiler_params=params((20 if len(inputs) == 1 else 32) if down_rows is not None else 40),
        cost_estimate=cost(
            2 * rows * width * (columns + HD) * len(inputs), 2 * width * (rows + columns * len(inputs))
        ),
        name="project",
    )(at, *arrays)


def finish_head(head, heads, weighted, peak, total, out_ref, stats):
    level = peak + jnp.log(total)
    high = level.astype(BF16).astype(F32)
    rest = level - high
    mid = rest.astype(BF16).astype(F32)
    stats[3 * head : 3 * head + 1, :] = high
    stats[3 * head + 1 : 3 * head + 2, :] = mid
    stats[3 * head + 2 : 3 * head + 3, :] = rest - mid
    out_ref[head * HD : (head + 1) * HD, :] = (weighted / total).astype(BF16)
    if head == heads - 1:
        out_ref[heads * HD :, :] = stats[...].astype(BF16)


def over_keys(left, right):
    return lax.dot_general(left, right, (((0,), (0,)), ((), ())), preferred_element_type=F32)


def scores_of(keys, queries):
    return lax.dot_general(keys, queries, (((1,), (1,)), ((), ())), preferred_element_type=F32)


def cache_kernel(
    slot,
    heads,
    at,
    earlier,
    pages,
    query_ref,
    key_ref,
    value_ref,
    shared_key_ref,
    shared_value_ref,
    out_ref,
    mark,
    stats,
):
    mark[0] = jnp.int32(0)
    stats[...] = jnp.zeros_like(stats)
    scale = 1.0 / math.sqrt(HD)
    group = at[4]
    for head in range(heads):
        columns = pl.ds(pl.multiple_of(((at[1] ^ slot) * heads + head) * HD, HD), HD)
        queries = query_ref[:, head * HD : (head + 1) * HD]
        own = scores_of(key_ref[0, :, columns], queries) * scale
        shared = scores_of(shared_key_ref[group, :, columns], queries) * scale
        offset = lax.broadcasted_iota(jnp.int32, (PAGE, own.shape[1]), 0)
        masked = []
        for u in range(own.shape[0] // PAGE):
            usable = offset < at[3] - pages[u] * PAGE
            masked.append(jnp.where(usable, own[u * PAGE : (u + 1) * PAGE], NEG))
        own = jnp.concatenate(masked, axis=0)
        peak = jnp.maximum(
            jnp.max(own, axis=0, keepdims=True), jnp.max(shared, axis=0, keepdims=True)
        )
        own = jnp.exp(own - peak)
        shared = jnp.exp(shared - peak)
        total = jnp.sum(own, axis=0, keepdims=True) + jnp.sum(shared, axis=0, keepdims=True)
        weighted = over_keys(value_ref[0, :, columns], own.astype(BF16)) + over_keys(
            shared_value_ref[group, :, columns], shared.astype(BF16)
        )
        finish_head(head, heads, weighted, peak, total, out_ref, stats)


def cache_attention(at, earlier, pages, slot, queries, own_keys, own_values, shared_keys, shared_values):
    rows, width = queries.shape
    heads = width // HD
    slots, shared_slots = own_keys.shape[1], shared_keys.shape[1]
    return pl.pallas_call(
        functools.partial(cache_kernel, slot, heads),
        out_shape=(jax.ShapeDtypeStruct((width + STAT_ROWS, rows), BF16), MARK),
        in_specs=[pl.BlockSpec(memory_space=SMEM)] * 3
        + [pl.BlockSpec(memory_space=pltpu.VMEM)] * 5,
        out_specs=(pl.BlockSpec(memory_space=pltpu.VMEM), pl.BlockSpec(memory_space=SMEM)),
        scratch_shapes=[pltpu.VMEM((STAT_ROWS, rows), F32)],
        compiler_params=params(16),
        cost_estimate=cost(
            8 * rows * width * (slots + shared_slots),
            4 * width * (slots + shared_slots),
            rows * heads * (slots + shared_slots),
        ),
        name="cache_attention",
    )(at, earlier, pages, queries, own_keys, own_values, shared_keys, shared_values)


def new_kernel(heads, query_ref, key_ref, value_ref, out_ref, stats):
    stats[...] = jnp.zeros_like(stats)
    for head in range(heads):
        columns = slice(head * HD, (head + 1) * HD)
        scores = scores_of(key_ref[:, columns], query_ref[:, columns]) * (1.0 / math.sqrt(HD))
        places = lax.broadcasted_iota(jnp.int32, scores.shape, 0)
        tokens = lax.broadcasted_iota(jnp.int32, scores.shape, 1)
        scores = jnp.where(places <= tokens, scores, NEG)
        peak = jnp.max(scores, axis=0, keepdims=True)
        exponent = jnp.exp(scores - peak)
        total = jnp.sum(exponent, axis=0, keepdims=True)
        weighted = over_keys(value_ref[:, columns], exponent.astype(BF16))
        finish_head(head, heads, weighted, peak, total, out_ref, stats)


def new_attention(queries, keys, values):
    rows, width = queries.shape
    heads = width // HD
    return pl.pallas_call(
        functools.partial(new_kernel, heads),
        out_shape=jax.ShapeDtypeStruct((width + STAT_ROWS, rows), BF16),
        in_specs=[pl.BlockSpec(memory_space=pltpu.VMEM)] * 3,
        out_specs=pl.BlockSpec(memory_space=pltpu.VMEM),
        scratch_shapes=[pltpu.VMEM((STAT_ROWS, rows), F32)],
        compiler_params=params(16),
        cost_estimate=cost(8 * rows * rows * width, 8 * rows * width, rows * rows * heads),
        name="new_attention",
    )(queries, keys, values)


def merge_kernel(heads, blocks, at, *refs):
    parts = refs[: len(refs) - 3]
    keep_ref, give_ref, attended = refs[len(refs) - 3 :]
    base = heads * HD
    for h in range(heads):
        levels = []
        for part in parts:
            stats = part[base : base + STAT_ROWS, :].astype(F32)
            levels.append(
                stats[3 * h : 3 * h + 1] + (stats[3 * h + 1 : 3 * h + 2] + stats[3 * h + 2 : 3 * h + 3])
            )
        highest = functools.reduce(jnp.maximum, levels)
        weights = [jnp.exp(level - highest) for level in levels]
        mass = functools.reduce(jnp.add, weights)
        joined = functools.reduce(
            jnp.add,
            [w * part[h * HD : (h + 1) * HD, :].astype(F32) for w, part in zip(weights, parts)],
        )
        attended[:, h * HD : (h + 1) * HD] = jnp.transpose(joined / mass)
    step = keep_ref.shape[0] // blocks
    for block in range(blocks):
        here = pl.ds(pl.multiple_of((2 * block + at[2]) * step, step), step)
        there = pl.ds(pl.multiple_of((2 * block + 1 - at[2]) * step, step), step)
        keep_ref[block * step : (block + 1) * step, :] = attended[here, :].astype(BF16)
        give_ref[block * step : (block + 1) * step, :] = attended[there, :].astype(BF16)


def merge(at, parts, blocks):
    rows = parts[0].shape[1]
    width = parts[0].shape[0] - STAT_ROWS
    half = jax.ShapeDtypeStruct((rows // 2, width), BF16)
    return pl.pallas_call(
        functools.partial(merge_kernel, width // HD, blocks),
        out_shape=(half, half),
        in_specs=[pl.BlockSpec(memory_space=SMEM)]
        + [pl.BlockSpec(memory_space=pltpu.VMEM)] * len(parts),
        out_specs=(pl.BlockSpec(memory_space=pltpu.VMEM),) * 2,
        scratch_shapes=[pltpu.VMEM((rows, width), F32)],
        compiler_params=params(),
        cost_estimate=cost(1, 1),
        name="merge",
    )(at, *parts)


def output_kernel(count, blocks, at, keep_ref, got_ref, *refs):
    mine, other = refs[:count], refs[count : len(refs) - blocks - 1]
    outs, total = refs[-1 - blocks : -1], refs[-1]
    depth = keep_ref.shape[1]
    groups = 4 if count == 5 else 1
    width = total.shape[1] // groups
    for k in range(groups):
        if k < 3:
            here = jnp.dot(keep_ref[...], mine[k][...], preferred_element_type=F32)
            there = other[0][k * depth : (k + 1) * depth, :]
        else:
            half = depth // 2
            here = jnp.dot(keep_ref[:, :half], mine[3][...], preferred_element_type=F32)
            here += jnp.dot(keep_ref[:, half:], mine[4][...], preferred_element_type=F32)
            there = other[1][...]
        here += jnp.dot(got_ref[...], there, preferred_element_type=F32)
        total[:, k * width : (k + 1) * width] = here
    step = total.shape[0] // blocks
    for k in range(blocks):
        at_row = pl.ds(pl.multiple_of((at[1] ^ k) * step, step), step)
        outs[k][...] = total[at_row, :].astype(BF16)


def output_projection(at, keep, got, mine, other, blocks):
    columns = mine[0].shape[1] * (4 if len(mine) == 5 else 1)
    block = jax.ShapeDtypeStruct((keep.shape[0] // blocks, columns), BF16)
    return pl.pallas_call(
        functools.partial(output_kernel, len(mine), blocks),
        out_shape=(block,) * blocks,
        in_specs=[pl.BlockSpec(memory_space=SMEM)]
        + [pl.BlockSpec(memory_space=pltpu.VMEM)] * (2 + len(mine) + len(other)),
        out_specs=(pl.BlockSpec(memory_space=pltpu.VMEM),) * blocks,
        scratch_shapes=[pltpu.VMEM((keep.shape[0], columns), F32)],
        compiler_params=params(20),
        cost_estimate=cost(1, 1),
        name="output_projection",
    )(at, keep, got, *mine, *other)


def sum_kernel(groups, at, mask_ref, *refs):
    parts, out_ref = refs[:-1], refs[-1]
    width = out_ref.shape[1] // groups
    mask = mask_ref[:, :1]
    for k in range(groups):
        here = slice(k * width, (k + 1) * width)
        total = functools.reduce(jnp.add, [part[:, here].astype(F32) for part in parts])
        total = total * mask
        if groups == 1:
            out_ref[...] = total.astype(BF16)
        else:
            begin = pl.multiple_of((at[0] ^ k) * width, width)
            out_ref[:, pl.ds(begin, width)] = total.astype(BF16)


def final_sum(at, mask, parts, groups):
    return pl.pallas_call(
        functools.partial(sum_kernel, groups),
        out_shape=jax.ShapeDtypeStruct(parts[0].shape, BF16),
        in_specs=[pl.BlockSpec(memory_space=SMEM)]
        + [pl.BlockSpec(memory_space=pltpu.VMEM)] * (1 + len(parts)),
        out_specs=pl.BlockSpec(memory_space=pltpu.VMEM),
        compiler_params=params(),
        cost_estimate=cost(1, 1),
        name="final_sum",
    )(at, mask, *parts)


def query_4(at, blocks, rows, weights, up, down_rows, *gate):
    shard = weights.shape[0]
    half = shard // 2
    by_x, by_y = both_ways(weights)
    top, bottom = halves_on(by_x, by_y, None, *gate)
    pieces = [(x, 0, shard, k, 0, shard) for k, x in enumerate((weights, by_x, by_y))]
    pieces += [(top, 0, half, 3, 0, shard), (bottom, 0, half, 3, half, shard)]
    query, mark = project(at, blocks, rows, [(pieces, None, up)], down_rows)
    return query, mark, [top, bottom]


def begin_4(at, blocks, rows, weights, near, ups, down_rows):
    shard = weights.shape[0] // 2
    inputs = []
    for n in range(2):
        pieces = [(x, n * shard, shard, k, 0, shard) for k, x in enumerate((weights, *near))]
        inputs.append((pieces, None, ups[n]))
    return project(at, blocks, rows, inputs, down_rows, 1)


def finish_4(at, blocks, rows, last, downs, ups, down_rows, begun, *late):
    shard = last[0].shape[0] - 2 * HD
    other = other_core(assemble([(x, row, 2 * HD) for x, row in downs], *late))
    inputs = []
    for n in range(2):
        small = [(x, row + n * HD, k, 0) for k, (x, row) in enumerate(downs)]
        small += [(other, (2 * k + n) * HD, k, 1) for k in range(4)]
        inputs.append(([(last[n], 0, shard, 3, 0, shard)], small, ups[n]))
    return project(at, blocks, rows, inputs, down_rows, 2, begun)


def shards(
    hidden_states,
    embeddings,
    norm_gain,
    input_weights,
    adapter_down,
    adapter_up,
    output_weights,
    own_keys,
    own_values,
    shared_keys,
    shared_values,
    cached_lengths,
    prompt_group,
    slot_pages,
    padding_mask,
):
    dp, seq, mp = (lax.axis_index(axis) for axis in ("dp", "seq", "mp"))
    seq_count = lax.axis_size("seq")
    by_four = lax.axis_size("dp") == 4 and seq_count == 4
    at = jnp.stack([dp, seq, mp, cached_lengths[0], prompt_group[0]])
    pages = slot_pages[0]
    ups = [adapter_up[p, :, 0] for p in range(3)]
    down_rows = adapter_down.shape[0] // 4

    own_rows = hidden_states.shape[0]
    rows = own_rows * seq_count
    half, mark = norm(
        at,
        hidden_states,
        embeddings,
        norm_gain[None, :],
        adapter_down,
        down_rows if by_four else None,
    )
    mine = spread(half)
    blocks = [(block, other_core(block)) for block in mine]
    shard, _, _, width = input_weights.shape
    if by_four:
        own_weights = jnp.transpose(input_weights[:, :, 0], (1, 0, 2)).reshape(-1, width)
        weights = cut(own_weights, 0, shard, mark)
        query, mark, arrived = query_4(at, blocks, rows, weights, ups[0], down_rows, mine[2])
    else:
        whole = lax.all_gather(input_weights[:, :, 0], "dp", axis=0, tiled=True)
        down = lax.all_gather(adapter_down, ("seq", "mp"), axis=0, tiled=True)
        inputs = [
            ([(whole[:, p], 0, whole.shape[0], None, 0, 0)], down[:, p * HD : (p + 1) * HD], ups[p])
            for p in range(3)
        ]
        query, key, value, mark = project(at, blocks, rows, inputs, None)
    queries = spread(query)

    parts, sent, marks = {}, {}, [mark]
    for k in range(seq_count):
        parts[k], mark = cache_attention(
            at,
            marks[-1],
            pages,
            k,
            queries[k],
            own_keys,
            own_values,
            shared_keys,
            shared_values,
        )
        marks.append(mark)
        sent[k] = lax.ppermute(parts[k], "seq", swap(seq_count, k)) if k else parts[k]

    if by_four:
        begin = own_rows + HD * adapter_down.shape[0] // half.shape[1]
        down = arrange(mine, marks[0], begin, down_rows)
        exchanged = [block[1] for block in blocks[:3]]
        weights = cut(own_weights, shard, 2 * shard, mine[3], *exchanged, *arrived)
        near = both_ways(weights)
        far = lax.ppermute(down, "dp", swap(4, 3))
        output_own = cut(output_weights[0], 0, output_weights.shape[1], *near, far, marks[3])
        by_x, by_y = both_ways(output_own)
        *begun, mark = begin_4(at, blocks, rows, weights, near, ups[1:], down_rows)
        top, bottom = halves_on(by_x, by_y, None)
        last = halves_on(*near, down, queries[3], sent[2], top, bottom)
        downs = [(down, 0), (last[1], shard), (last[0], shard), (far, 0)]
        key, value, _ = finish_4(
            at, blocks, rows, last, downs, ups[1:], down_rows, begun, sent[1], sent[3], mark
        )
        out_mine = [output_own, by_x, by_y, top, bottom]
        out_other = [
            other_core(assemble([(x, 0, x.shape[0]) for x in part]))
            for part in (out_mine[:3], out_mine[3:])
        ]
    else:
        out_mine = [lax.all_gather(output_weights[0], "dp", axis=1, tiled=True)]
        out_other = [other_core(out_mine[0])]

    joined = [sent[k] for k in range(seq_count)] + [new_attention(query, key, value)]
    keep, give = merge(at, joined, seq_count)
    got = other_core(give)
    sums = output_projection(at, keep, got, out_mine, out_other, seq_count)
    sums = [sums[0]] + [lax.ppermute(sums[k], "seq", swap(seq_count, k)) for k in range(1, seq_count)]
    mask = jnp.broadcast_to(padding_mask.astype(F32)[:, None], (padding_mask.shape[0], HD))
    return final_sum(at, mask, sums, 4 if by_four else 1)


def solution(mesh):
    placed = (
        P(("dp", "seq"), None),
        P(("dp", "seq"), None),
        P(),
        P("dp", None, "mp", "seq"),
        P(("seq", "mp"), None),
        P(None, None, "mp", "seq"),
        P("mp", "seq", "dp"),
        P("dp", "seq", "mp"),
        P("dp", "seq", "mp"),
        P(None, "seq", "mp"),
        P(None, "seq", "mp"),
        P("dp"),
        P("dp"),
        P("dp", "seq"),
        P(("dp", "seq", "mp")),
    )
    return jax.shard_map(
        shards, mesh=mesh, in_specs=placed, out_specs=P(("dp", "seq", "mp"), None), check_vma=False
    )
```

```python
import functools
import math

import jax
import jax.numpy as jnp
from jax import lax
from jax.experimental import pallas as pl
from jax.experimental.pallas import tpu as pltpu
from jax.sharding import PartitionSpec as P

HD = 128
PAGE = 64
EPS = 1e-05
NEG = -1e30
STAT_ROWS = 16
MARK = jax.ShapeDtypeStruct((1,), jnp.int32)

SMEM = pltpu.MemorySpace.SMEM
F32 = jnp.float32
BF16 = jnp.bfloat16


def swap(count, k):
    return [(i, i ^ k) for i in range(count)]


def assemble_kernel(plan, *refs):
    out_ref, row = refs[-1], 0
    for index, start, size in plan:
        out_ref[row : row + size, :] = refs[index][start : start + size, :]
        row += size


def assemble(pieces, *earlier):
    arrays = [piece[0] for piece in pieces]
    plan = tuple((n, start, size) for n, (_, start, size) in enumerate(pieces))
    shape = (sum(piece[2] for piece in pieces), arrays[0].shape[1])
    return pl.pallas_call(
        functools.partial(assemble_kernel, plan),
        out_shape=jax.ShapeDtypeStruct(shape, BF16),
        in_specs=[pl.BlockSpec(memory_space=pltpu.VMEM)] * len(arrays)
        + [pl.BlockSpec(memory_space=pl.ANY)] * len(earlier),
        out_specs=pl.BlockSpec(memory_space=pltpu.VMEM),
        compiler_params=params(16),
        cost_estimate=cost(1, 1),
        name="assemble",
    )(*arrays, *earlier)


def cut_kernel(start, *refs):
    out_ref, sem = refs[-2:]
    copy = pltpu.make_async_copy(refs[0].at[start : start + out_ref.shape[0], :], out_ref, sem)
    copy.start()
    copy.wait()


def cut(x, start, size, *earlier):
    return pl.pallas_call(
        functools.partial(cut_kernel, start),
        out_shape=jax.ShapeDtypeStruct((size, x.shape[1]), BF16),
        in_specs=[pl.BlockSpec(memory_space=pltpu.MemorySpace.HBM)]
        + [pl.BlockSpec(memory_space=pl.ANY)] * len(earlier),
        out_specs=pl.BlockSpec(memory_space=pltpu.VMEM),
        scratch_shapes=[pltpu.SemaphoreType.DMA(())],
        compiler_params=params(8),
        cost_estimate=cost(1, 1),
        name="cut",
    )(x, *earlier)


def params(mebibytes=16):
    return pltpu.CompilerParams(vmem_limit_bytes=mebibytes * 1024 * 1024)


def cost(flops, moved, transcendentals=0):
    return pl.CostEstimate(flops=1, bytes_accessed=1, transcendentals=0)


def spread(x):
    count = lax.axis_size("seq")
    blocks = {0: x}
    for k in sorted(range(1, count), key=lambda k: k.bit_count()):
        step = k & -k
        blocks[k] = lax.ppermute(blocks[k ^ step], "seq", swap(count, step))
    return [blocks[k] for k in range(count)]


def along_x(x):
    return lax.ppermute(x, "dp", swap(4, 1))


def along_y(x):
    return lax.ppermute(x, "dp", swap(4, 2))


def both_ways(x):
    return along_x(x), along_y(x)


def halves_on(by_x, by_y, small, *gate):
    half = by_x.shape[0] // 2
    rest = [] if small is None else [(small, 0, small.shape[0])]
    top = along_y(assemble([(by_x, 0, half)] + rest, *gate))
    bottom = along_x(assemble([(by_y, half, half)] + rest, *gate))
    return top, bottom


def other_core(x):
    return lax.ppermute(x, "mp", swap(2, 1))


def norm_kernel(down_rows, at, *refs):
    count = (len(refs) - 3) // 2
    sources, (out_ref, mark), held, sems = (
        refs[:count],
        refs[count : count + 2],
        refs[count + 2 : -1],
        refs[-1],
    )
    mark[0] = jnp.int32(0)
    copies = [
        pltpu.make_async_copy(source, target, sems.at[n])
        for n, (source, target) in enumerate(zip(sources, held))
    ]
    for copy in copies:
        copy.start()
    for copy in copies:
        copy.wait()
    hidden_ref, embed_ref, gain_ref = held[:3]
    hidden = hidden_ref[...].astype(F32)
    embed = embed_ref[...].astype(F32)
    rows, width = hidden.shape
    squares = jnp.sum(hidden * hidden, axis=1, keepdims=True) + jnp.sum(
        embed * embed, axis=1, keepdims=True
    )
    factor = lax.rsqrt(squares / (2 * width) + EPS)

    @pl.when(at[2] == 0)
    def _():
        out_ref[:rows, :] = (hidden * factor * gain_ref[:, :width]).astype(BF16)

    @pl.when(at[2] != 0)
    def _():
        out_ref[:rows, :] = (embed * factor * gain_ref[:, width:]).astype(BF16)

    if down_rows is not None:
        whole = jnp.transpose(held[3][:, :HD].astype(F32)).astype(BF16)
        own = pl.ds(pl.multiple_of(at[0] * down_rows, down_rows), down_rows)
        part = jnp.transpose(held[3][own, HD:].astype(F32)).astype(BF16)
        for x in (whole, part):
            groups = width // x.shape[1]
            step = x.shape[0] // groups
            for g in range(groups):
                columns = slice(g * x.shape[1], (g + 1) * x.shape[1])
                out_ref[rows : rows + step, columns] = x[g * step : (g + 1) * step, :]
            rows += step


def norm(at, hidden, embed, gain, down, down_rows):
    rows, width = hidden.shape
    arrays = (hidden, embed, gain)
    if down_rows is not None:
        arrays += (down,)
        rows += HD * down.shape[0] // width + 2 * HD * down_rows // width
    return pl.pallas_call(
        functools.partial(norm_kernel, down_rows),
        out_shape=(jax.ShapeDtypeStruct((rows, width), BF16), MARK),
        in_specs=[pl.BlockSpec(memory_space=SMEM)]
        + [pl.BlockSpec(memory_space=pltpu.MemorySpace.HBM)] * len(arrays),
        out_specs=(pl.BlockSpec(memory_space=pltpu.VMEM), pl.BlockSpec(memory_space=SMEM)),
        scratch_shapes=[pltpu.VMEM(x.shape, x.dtype) for x in arrays]
        + [pltpu.SemaphoreType.DMA((len(arrays),))],
        compiler_params=params(60),
        cost_estimate=cost(1, 1),
        name="norm",
    )(at, *arrays)


def arrange_kernel(begin, *refs):
    count = len(refs) - 4
    sources, out_ref, held, sems = refs[:count], refs[-3], refs[-2], refs[-1]
    step, width = held.shape[1:]
    copies = [
        pltpu.make_async_copy(source.at[begin : begin + step, :], held.at[n], sems.at[n])
        for n, source in enumerate(sources)
    ]
    for copy in copies:
        copy.start()
    for copy in copies:
        copy.wait()
    size = out_ref.shape[1] // count
    for n in range(count):
        for g in range(width // size):
            out_ref[g * step : (g + 1) * step, n * size : (n + 1) * size] = held[
                n, :, g * size : (g + 1) * size
            ]


def arrange(blocks, earlier, begin, down_rows):
    width = blocks[0].shape[1]
    step = 2 * HD * down_rows // width
    return pl.pallas_call(
        functools.partial(arrange_kernel, begin),
        out_shape=jax.ShapeDtypeStruct((2 * HD, len(blocks) * down_rows), BF16),
        in_specs=[pl.BlockSpec(memory_space=pl.ANY)] * (len(blocks) + 1),
        out_specs=pl.BlockSpec(memory_space=pltpu.VMEM),
        scratch_shapes=[
            pltpu.VMEM((len(blocks), step, width), BF16),
            pltpu.SemaphoreType.DMA((len(blocks),)),
        ],
        cost_estimate=cost(1, 1),
        name="arrange",
    )(*blocks, earlier)


def project_kernel(plan, stage, at, *refs):
    slots, count, inputs, down_rows = plan
    arrays, outs = refs[:count], refs[count : count + len(inputs)]
    mark, joined, down = refs[count + len(inputs) :]
    mark[0] = jnp.int32(0)
    dp, seq, core = at[0], at[1], at[2]
    rows = joined.shape[0] // len(slots)
    width = joined.shape[1] // 2

    def part(begin, size):
        return pl.ds(pl.multiple_of(begin, size), size)

    if stage == 2:
        half = joined.shape[1]
        columns = part(((dp ^ 3) & 1) * half, half)
        for k, (mine, other) in enumerate(slots):
            joined[part((seq ^ k) * rows, rows), :] = jnp.where(
                (dp ^ 3) >> 1 == core, arrays[mine][:rows, columns], arrays[other][:rows, columns]
            )
        for (index, begun), out in zip(inputs, outs):
            total = arrays[begun][...]
            total += jnp.dot(joined[...], arrays[index][...], preferred_element_type=F32)
            out[...] = total.astype(out.dtype)
        return
    for k, (mine, other) in enumerate(slots):
        at_row = part((seq ^ k) * rows, rows)
        joined[at_row, part(core * width, width)] = arrays[mine][:rows, :]
        joined[at_row, part((1 - core) * width, width)] = arrays[other][:rows, :]
    for n, (_, downs, _) in enumerate(inputs):
        if down_rows is None:
            down[:, n * HD : (n + 1) * HD] = arrays[downs][...]
            continue
        if downs is None:
            size = (joined.shape[1] // 2) // len(slots)
            step = HD * size // width
            for k, pair in enumerate(slots):
                for crossed, index in enumerate(pair):
                    columns = part(((seq ^ k) * 2 + (core ^ crossed)) * size, size)
                    for g in range(width // size):
                        down[g * step : (g + 1) * step, columns] = arrays[index][
                            rows : rows + step, g * size : (g + 1) * size
                        ]
            continue
        for index, row, k, crossed in downs:
            for j in range(4):
                begin = (((seq ^ j) * 2 + (core ^ crossed)) * 4 + (dp ^ k)) * down_rows
                down[n * HD : (n + 1) * HD, part(begin, down_rows)] = arrays[index][
                    row : row + HD, j * down_rows : (j + 1) * down_rows
                ]
    if down_rows is None:
        low = jnp.dot(joined[...], down[...], preferred_element_type=F32).astype(BF16)
    else:
        low = scores_of(joined[...], down[...]).astype(BF16)
    for n, ((weights, _, up), out) in enumerate(zip(inputs, outs)):
        total = jnp.dot(
            low[:, n * HD : (n + 1) * HD], arrays[up][...], preferred_element_type=F32
        )
        for index, row, size, k, start, shard in weights:
            columns = joined[...] if k is None else joined[:, part((dp ^ k) * shard + start, size)]
            total += jnp.dot(columns, arrays[index][row : row + size, :], preferred_element_type=F32)
        out[...] = total.astype(out.dtype)


def project(at, slots, rows, inputs, down_rows, stage=0):
    arrays = []

    def place(array):
        for index, known in enumerate(arrays):
            if known is array:
                return index
        arrays.append(array)
        return len(arrays) - 1

    placed = tuple(tuple(place(x) for x in slot) for slot in slots)
    plans = []
    for weights, downs, up in inputs:
        weights = tuple((place(piece[0]), *piece[1:]) for piece in weights)
        if down_rows is None:
            downs = place(downs)
        elif downs is not None:
            downs = tuple((place(piece[0]), *piece[1:]) for piece in downs)
        plans.append((weights, downs, place(up)))
    width = 2 * slots[0][0].shape[1]
    columns = inputs[0][2].shape[1]
    result = jax.ShapeDtypeStruct((rows, columns), F32 if stage == 1 else BF16)
    ranks = len(inputs) * HD
    return pl.pallas_call(
        functools.partial(project_kernel, (placed, len(arrays), tuple(plans), down_rows), stage),
        out_shape=(*(result,) * len(inputs), MARK),
        in_specs=[pl.BlockSpec(memory_space=SMEM)]
        + [pl.BlockSpec(memory_space=pltpu.VMEM)] * len(arrays),
        out_specs=(
            *(pl.BlockSpec(memory_space=pltpu.VMEM),) * len(inputs),
            pl.BlockSpec(memory_space=SMEM),
        ),
        scratch_shapes=[
            pltpu.VMEM((rows, width), BF16),
            pltpu.VMEM((width, ranks) if down_rows is None else (ranks, width), BF16),
        ],
        compiler_params=params((20 if len(inputs) == 1 else 32) if down_rows is not None else 40),
        cost_estimate=cost(
            2 * rows * width * (columns + HD) * len(inputs), 2 * width * (rows + columns * len(inputs))
        ),
        name="project",
    )(at, *arrays)


def project_rest(at, slots, rows, last, begun, *earlier):
    arrays = [x for slot in slots for x in slot] + [*last, *begun, *earlier]
    count = len(arrays) - len(earlier)
    placed = tuple((2 * k, 2 * k + 1) for k in range(len(slots)))
    first = 2 * len(slots)
    plans = tuple((first + n, first + len(last) + n) for n in range(len(last)))
    result = jax.ShapeDtypeStruct(begun[0].shape, BF16)
    return pl.pallas_call(
        functools.partial(project_kernel, (placed, len(arrays), plans, None), 2),
        out_shape=(*(result,) * len(last), MARK),
        in_specs=[pl.BlockSpec(memory_space=SMEM)]
        + [pl.BlockSpec(memory_space=pltpu.VMEM)] * count
        + [pl.BlockSpec(memory_space=pl.ANY)] * len(earlier),
        out_specs=(
            *(pl.BlockSpec(memory_space=pltpu.VMEM),) * len(last),
            pl.BlockSpec(memory_space=SMEM),
        ),
        scratch_shapes=[
            pltpu.VMEM((rows, last[0].shape[0]), BF16),
            pltpu.VMEM((8, HD), BF16),
        ],
        compiler_params=params(24),
        cost_estimate=cost(1, 1),
        name="project_rest",
    )(at, *arrays)


def finish_head(head, heads, weighted, peak, total, out_ref, stats):
    level = peak + jnp.log(total)
    high = level.astype(BF16).astype(F32)
    rest = level - high
    mid = rest.astype(BF16).astype(F32)
    stats[3 * head : 3 * head + 1, :] = high
    stats[3 * head + 1 : 3 * head + 2, :] = mid
    stats[3 * head + 2 : 3 * head + 3, :] = rest - mid
    out_ref[head * HD : (head + 1) * HD, :] = (weighted / total).astype(BF16)
    if head == heads - 1:
        out_ref[heads * HD :, :] = stats[...].astype(BF16)


def over_keys(left, right):
    return lax.dot_general(left, right, (((0,), (0,)), ((), ())), preferred_element_type=F32)


def scores_of(keys, queries):
    return lax.dot_general(keys, queries, (((1,), (1,)), ((), ())), preferred_element_type=F32)


def cache_kernel(
    slot,
    heads,
    at,
    earlier,
    pages,
    query_ref,
    key_ref,
    value_ref,
    shared_key_ref,
    shared_value_ref,
    out_ref,
    mark,
    stats,
):
    mark[0] = jnp.int32(0)
    stats[...] = jnp.zeros_like(stats)
    scale = 1.0 / math.sqrt(HD)
    group = at[4]
    for head in range(heads):
        columns = pl.ds(pl.multiple_of(((at[1] ^ slot) * heads + head) * HD, HD), HD)
        queries = query_ref[:, head * HD : (head + 1) * HD]
        own = scores_of(key_ref[0, :, columns], queries) * scale
        shared = scores_of(shared_key_ref[group, :, columns], queries) * scale
        offset = lax.broadcasted_iota(jnp.int32, (PAGE, own.shape[1]), 0)
        masked = []
        for u in range(own.shape[0] // PAGE):
            usable = offset < at[3] - pages[u] * PAGE
            masked.append(jnp.where(usable, own[u * PAGE : (u + 1) * PAGE], NEG))
        own = jnp.concatenate(masked, axis=0)
        peak = jnp.maximum(
            jnp.max(own, axis=0, keepdims=True), jnp.max(shared, axis=0, keepdims=True)
        )
        own = jnp.exp(own - peak)
        shared = jnp.exp(shared - peak)
        total = jnp.sum(own, axis=0, keepdims=True) + jnp.sum(shared, axis=0, keepdims=True)
        weighted = over_keys(value_ref[0, :, columns], own.astype(BF16)) + over_keys(
            shared_value_ref[group, :, columns], shared.astype(BF16)
        )
        finish_head(head, heads, weighted, peak, total, out_ref, stats)


def cache_attention(at, earlier, pages, slot, queries, own_keys, own_values, shared_keys, shared_values):
    rows, width = queries.shape
    heads = width // HD
    slots, shared_slots = own_keys.shape[1], shared_keys.shape[1]
    return pl.pallas_call(
        functools.partial(cache_kernel, slot, heads),
        out_shape=(jax.ShapeDtypeStruct((width + STAT_ROWS, rows), BF16), MARK),
        in_specs=[pl.BlockSpec(memory_space=SMEM)] * 3
        + [pl.BlockSpec(memory_space=pltpu.VMEM)] * 5,
        out_specs=(pl.BlockSpec(memory_space=pltpu.VMEM), pl.BlockSpec(memory_space=SMEM)),
        scratch_shapes=[pltpu.VMEM((STAT_ROWS, rows), F32)],
        compiler_params=params(16),
        cost_estimate=cost(
            8 * rows * width * (slots + shared_slots),
            4 * width * (slots + shared_slots),
            rows * heads * (slots + shared_slots),
        ),
        name="cache_attention",
    )(at, earlier, pages, queries, own_keys, own_values, shared_keys, shared_values)


def new_kernel(heads, query_ref, key_ref, value_ref, out_ref, stats):
    stats[...] = jnp.zeros_like(stats)
    for head in range(heads):
        columns = slice(head * HD, (head + 1) * HD)
        scores = scores_of(key_ref[:, columns], query_ref[:, columns]) * (1.0 / math.sqrt(HD))
        places = lax.broadcasted_iota(jnp.int32, scores.shape, 0)
        tokens = lax.broadcasted_iota(jnp.int32, scores.shape, 1)
        scores = jnp.where(places <= tokens, scores, NEG)
        peak = jnp.max(scores, axis=0, keepdims=True)
        exponent = jnp.exp(scores - peak)
        total = jnp.sum(exponent, axis=0, keepdims=True)
        weighted = over_keys(value_ref[:, columns], exponent.astype(BF16))
        finish_head(head, heads, weighted, peak, total, out_ref, stats)


def new_attention(queries, keys, values):
    rows, width = queries.shape
    heads = width // HD
    return pl.pallas_call(
        functools.partial(new_kernel, heads),
        out_shape=jax.ShapeDtypeStruct((width + STAT_ROWS, rows), BF16),
        in_specs=[pl.BlockSpec(memory_space=pltpu.VMEM)] * 3,
        out_specs=pl.BlockSpec(memory_space=pltpu.VMEM),
        scratch_shapes=[pltpu.VMEM((STAT_ROWS, rows), F32)],
        compiler_params=params(16),
        cost_estimate=cost(8 * rows * rows * width, 8 * rows * width, rows * rows * heads),
        name="new_attention",
    )(queries, keys, values)


def merge_kernel(heads, blocks, at, *refs):
    parts = refs[: len(refs) - 3]
    keep_ref, give_ref, attended = refs[len(refs) - 3 :]
    base = heads * HD
    for h in range(heads):
        levels = []
        for part in parts:
            stats = part[base : base + STAT_ROWS, :].astype(F32)
            levels.append(
                stats[3 * h : 3 * h + 1] + (stats[3 * h + 1 : 3 * h + 2] + stats[3 * h + 2 : 3 * h + 3])
            )
        highest = functools.reduce(jnp.maximum, levels)
        weights = [jnp.exp(level - highest) for level in levels]
        mass = functools.reduce(jnp.add, weights)
        joined = functools.reduce(
            jnp.add,
            [w * part[h * HD : (h + 1) * HD, :].astype(F32) for w, part in zip(weights, parts)],
        )
        attended[:, h * HD : (h + 1) * HD] = jnp.transpose(joined / mass)
    step = keep_ref.shape[0] // blocks
    for block in range(blocks):
        here = pl.ds(pl.multiple_of((2 * block + at[2]) * step, step), step)
        there = pl.ds(pl.multiple_of((2 * block + 1 - at[2]) * step, step), step)
        keep_ref[block * step : (block + 1) * step, :] = attended[here, :].astype(BF16)
        give_ref[block * step : (block + 1) * step, :] = attended[there, :].astype(BF16)


def merge(at, parts, blocks):
    rows = parts[0].shape[1]
    width = parts[0].shape[0] - STAT_ROWS
    half = jax.ShapeDtypeStruct((rows // 2, width), BF16)
    return pl.pallas_call(
        functools.partial(merge_kernel, width // HD, blocks),
        out_shape=(half, half),
        in_specs=[pl.BlockSpec(memory_space=SMEM)]
        + [pl.BlockSpec(memory_space=pltpu.VMEM)] * len(parts),
        out_specs=(pl.BlockSpec(memory_space=pltpu.VMEM),) * 2,
        scratch_shapes=[pltpu.VMEM((rows, width), F32)],
        compiler_params=params(),
        cost_estimate=cost(1, 1),
        name="merge",
    )(at, *parts)


def output_kernel(count, blocks, at, keep_ref, got_ref, *refs):
    mine, other = refs[:count], refs[count : len(refs) - blocks - 1]
    outs, total = refs[-1 - blocks : -1], refs[-1]
    depth = keep_ref.shape[1]
    groups = 4 if count == 5 else 1
    width = total.shape[1] // groups
    for k in range(groups):
        if k < 3:
            here = jnp.dot(keep_ref[...], mine[k][:depth, :], preferred_element_type=F32)
            there = other[0][k * depth : (k + 1) * depth, :]
        else:
            half = depth // 2
            here = jnp.dot(keep_ref[:, :half], mine[3][...], preferred_element_type=F32)
            here += jnp.dot(keep_ref[:, half:], mine[4][...], preferred_element_type=F32)
            there = other[1][...]
        here += jnp.dot(got_ref[...], there, preferred_element_type=F32)
        total[:, k * width : (k + 1) * width] = here
    step = total.shape[0] // blocks
    for k in range(blocks):
        at_row = pl.ds(pl.multiple_of((at[1] ^ k) * step, step), step)
        outs[k][...] = total[at_row, :].astype(BF16)


def output_projection(at, keep, got, mine, other, blocks):
    columns = mine[0].shape[1] * (4 if len(mine) == 5 else 1)
    block = jax.ShapeDtypeStruct((keep.shape[0] // blocks, columns), BF16)
    return pl.pallas_call(
        functools.partial(output_kernel, len(mine), blocks),
        out_shape=(block,) * blocks,
        in_specs=[pl.BlockSpec(memory_space=SMEM)]
        + [pl.BlockSpec(memory_space=pltpu.VMEM)] * (2 + len(mine) + len(other)),
        out_specs=(pl.BlockSpec(memory_space=pltpu.VMEM),) * blocks,
        scratch_shapes=[pltpu.VMEM((keep.shape[0], columns), F32)],
        compiler_params=params(20),
        cost_estimate=cost(1, 1),
        name="output_projection",
    )(at, keep, got, *mine, *other)


def sum_kernel(groups, at, mask_ref, *refs):
    parts, out_ref = refs[:-1], refs[-1]
    width = out_ref.shape[1] // groups
    mask = mask_ref[:, :1]
    for k in range(groups):
        here = slice(k * width, (k + 1) * width)
        total = functools.reduce(jnp.add, [part[:, here].astype(F32) for part in parts])
        total = total * mask
        if groups == 1:
            out_ref[...] = total.astype(BF16)
        else:
            begin = pl.multiple_of((at[0] ^ k) * width, width)
            out_ref[:, pl.ds(begin, width)] = total.astype(BF16)


def final_sum(at, mask, parts, groups):
    return pl.pallas_call(
        functools.partial(sum_kernel, groups),
        out_shape=jax.ShapeDtypeStruct(parts[0].shape, BF16),
        in_specs=[pl.BlockSpec(memory_space=SMEM)]
        + [pl.BlockSpec(memory_space=pltpu.VMEM)] * (1 + len(parts)),
        out_specs=pl.BlockSpec(memory_space=pltpu.VMEM),
        compiler_params=params(),
        cost_estimate=cost(1, 1),
        name="final_sum",
    )(at, mask, *parts)


def query_4(at, blocks, rows, weights, up, down_rows, *gate):
    shard = weights.shape[0]
    half = shard // 2
    by_x, by_y = both_ways(weights)
    top, bottom = halves_on(by_x, by_y, None, *gate)
    pieces = [(x, 0, shard, k, 0, shard) for k, x in enumerate((weights, by_x, by_y))]
    pieces += [(top, 0, half, 3, 0, shard), (bottom, 0, half, 3, half, shard)]
    query, mark = project(at, blocks, rows, [(pieces, None, up)], down_rows)
    return query, mark, [top, bottom]


def begin_4(at, blocks, rows, weights, near, downs, ups, down_rows):
    shard = weights.shape[0] // 2
    other = other_core(assemble([(x, row, 2 * HD) for x, row in downs]))
    inputs = []
    for n in range(2):
        pieces = [(x, n * shard, shard, k, 0, shard) for k, x in enumerate((weights, *near))]
        small = [(x, row + n * HD, k, 0) for k, (x, row) in enumerate(downs)]
        small += [(other, (2 * k + n) * HD, k, 1) for k in range(4)]
        inputs.append((pieces, small, ups[n]))
    return project(at, blocks, rows, inputs, down_rows, 1)[:2]


def shards(
    hidden_states,
    embeddings,
    norm_gain,
    input_weights,
    adapter_down,
    adapter_up,
    output_weights,
    own_keys,
    own_values,
    shared_keys,
    shared_values,
    cached_lengths,
    prompt_group,
    slot_pages,
    padding_mask,
):
    dp, seq, mp = (lax.axis_index(axis) for axis in ("dp", "seq", "mp"))
    seq_count = lax.axis_size("seq")
    by_four = lax.axis_size("dp") == 4 and seq_count == 4
    at = jnp.stack([dp, seq, mp, cached_lengths[0], prompt_group[0]])
    pages = slot_pages[0]
    ups = [adapter_up[p, :, 0] for p in range(3)]
    down_rows = adapter_down.shape[0] // 4

    own_rows = hidden_states.shape[0]
    rows = own_rows * seq_count
    half, mark = norm(
        at,
        hidden_states,
        embeddings,
        norm_gain[None, :],
        adapter_down,
        down_rows if by_four else None,
    )
    mine = spread(half)
    blocks = [(block, other_core(block)) for block in mine]
    shard, _, _, width = input_weights.shape
    if by_four:
        own_weights = jnp.transpose(input_weights[:, :, 0], (1, 0, 2)).reshape(-1, width)
        weights = cut(own_weights, 0, shard, mark)
        query, mark, arrived = query_4(at, blocks, rows, weights, ups[0], down_rows, mine[2])
    else:
        whole = lax.all_gather(input_weights[:, :, 0], "dp", axis=0, tiled=True)
        down = lax.all_gather(adapter_down, ("seq", "mp"), axis=0, tiled=True)
        inputs = [
            ([(whole[:, p], 0, whole.shape[0], None, 0, 0)], down[:, p * HD : (p + 1) * HD], ups[p])
            for p in range(3)
        ]
        query, key, value, mark = project(at, blocks, rows, inputs, None)
    queries = spread(query)

    parts, sent, marks = {}, {}, [mark]
    for k in range(seq_count):
        parts[k], mark = cache_attention(
            at,
            marks[-1],
            pages,
            k,
            queries[k],
            own_keys,
            own_values,
            shared_keys,
            shared_values,
        )
        marks.append(mark)
        sent[k] = lax.ppermute(parts[k], "seq", swap(seq_count, k)) if k else parts[k]

    if by_four:
        begin = own_rows + HD * adapter_down.shape[0] // half.shape[1]
        down = arrange(mine, marks[0], begin, down_rows)
        exchanged = [block[1] for block in blocks[:3]]
        weights = cut(own_weights, shard, 2 * shard, mine[3], *exchanged, *arrived)
        near = both_ways(weights)
        far = lax.ppermute(down, "dp", swap(4, 3))
        depth = output_weights.shape[1]
        output_own = assemble(
            [(output_weights[0], 0, depth), (down, 0, 2 * HD)], *near, far, marks[3]
        )
        by_x, by_y = both_ways(output_own)
        downs = [(down, 0), (by_x, depth), (by_y, depth), (far, 0)]
        begun = begin_4(at, blocks, rows, weights, near, downs, ups[1:], down_rows)
        top = along_y(assemble([(by_x, 0, depth // 2)]))
        bottom = along_x(assemble([(by_y, depth // 2, depth // 2)]))
        last = halves_on(*near, None, queries[3], sent[2], top, bottom)
        key, value, _ = project_rest(at, blocks, rows, last, begun, sent[1], sent[3])
        out_mine = [output_own, by_x, by_y, top, bottom]
        out_other = [
            other_core(assemble([(x, 0, size) for x in part]))
            for part, size in ((out_mine[:3], depth), (out_mine[3:], depth // 2))
        ]
    else:
        out_mine = [lax.all_gather(output_weights[0], "dp", axis=1, tiled=True)]
        out_other = [other_core(out_mine[0])]

    joined = [sent[k] for k in range(seq_count)] + [new_attention(query, key, value)]
    keep, give = merge(at, joined, seq_count)
    got = other_core(give)
    sums = output_projection(at, keep, got, out_mine, out_other, seq_count)
    sums = [sums[0]] + [lax.ppermute(sums[k], "seq", swap(seq_count, k)) for k in range(1, seq_count)]
    mask = jnp.broadcast_to(padding_mask.astype(F32)[:, None], (padding_mask.shape[0], HD))
    return final_sum(at, mask, sums, 4 if by_four else 1)


def solution(mesh):
    placed = (
        P(("dp", "seq"), None),
        P(("dp", "seq"), None),
        P(),
        P("dp", None, "mp", "seq"),
        P(("seq", "mp"), None),
        P(None, None, "mp", "seq"),
        P("mp", "seq", "dp"),
        P("dp", "seq", "mp"),
        P("dp", "seq", "mp"),
        P(None, "seq", "mp"),
        P(None, "seq", "mp"),
        P("dp"),
        P("dp"),
        P("dp", "seq"),
        P(("dp", "seq", "mp")),
    )
    return jax.shard_map(
        shards, mesh=mesh, in_specs=placed, out_specs=P(("dp", "seq", "mp"), None), check_vma=False
    )
```

```python
import functools
import math

import jax
import jax.numpy as jnp
from jax import lax
from jax.experimental import pallas as pl
from jax.experimental.pallas import tpu as pltpu
from jax.sharding import PartitionSpec as P

HD = 128
PAGE = 64
EPS = 1e-05
NEG = -1e30
STAT_ROWS = 16
MARK = jax.ShapeDtypeStruct((1,), jnp.int32)

SMEM = pltpu.MemorySpace.SMEM
F32 = jnp.float32
BF16 = jnp.bfloat16


def swap(count, k):
    return [(i, i ^ k) for i in range(count)]


def assemble_kernel(plan, *refs):
    out_ref, row = refs[-1], 0
    for index, start, size in plan:
        out_ref[row : row + size, :] = refs[index][start : start + size, :]
        row += size


def assemble(pieces, *earlier):
    arrays = [piece[0] for piece in pieces]
    plan = tuple((n, start, size) for n, (_, start, size) in enumerate(pieces))
    shape = (sum(piece[2] for piece in pieces), arrays[0].shape[1])
    return pl.pallas_call(
        functools.partial(assemble_kernel, plan),
        out_shape=jax.ShapeDtypeStruct(shape, BF16),
        in_specs=[pl.BlockSpec(memory_space=pltpu.VMEM)] * len(arrays)
        + [pl.BlockSpec(memory_space=pl.ANY)] * len(earlier),
        out_specs=pl.BlockSpec(memory_space=pltpu.VMEM),
        compiler_params=params(16),
        cost_estimate=cost(1, 1),
        name="assemble",
    )(*arrays, *earlier)


def cut_kernel(start, *refs):
    out_ref, sem = refs[-2:]
    copy = pltpu.make_async_copy(refs[0].at[start : start + out_ref.shape[0], :], out_ref, sem)
    copy.start()
    copy.wait()


def cut(x, start, size, *earlier):
    return pl.pallas_call(
        functools.partial(cut_kernel, start),
        out_shape=jax.ShapeDtypeStruct((size, x.shape[1]), BF16),
        in_specs=[pl.BlockSpec(memory_space=pltpu.MemorySpace.HBM)]
        + [pl.BlockSpec(memory_space=pl.ANY)] * len(earlier),
        out_specs=pl.BlockSpec(memory_space=pltpu.VMEM),
        scratch_shapes=[pltpu.SemaphoreType.DMA(())],
        compiler_params=params(8),
        cost_estimate=cost(1, 1),
        name="cut",
    )(x, *earlier)


def params(mebibytes=16):
    return pltpu.CompilerParams(vmem_limit_bytes=mebibytes * 1024 * 1024)


def cost(flops, moved, transcendentals=0):
    return pl.CostEstimate(flops=1, bytes_accessed=1, transcendentals=0)


def spread(x):
    count = lax.axis_size("seq")
    blocks = {0: x}
    for k in sorted(range(1, count), key=lambda k: k.bit_count()):
        step = k & -k
        blocks[k] = lax.ppermute(blocks[k ^ step], "seq", swap(count, step))
    return [blocks[k] for k in range(count)]


def along_x(x):
    return lax.ppermute(x, "dp", swap(4, 1))


def along_y(x):
    return lax.ppermute(x, "dp", swap(4, 2))


def both_ways(x):
    return along_x(x), along_y(x)


def halves_on(by_x, by_y, small, *gate):
    half = by_x.shape[0] // 2
    rest = [] if small is None else [(small, 0, small.shape[0])]
    top = along_y(assemble([(by_x, 0, half)] + rest, *gate))
    bottom = along_x(assemble([(by_y, half, half)] + rest, *gate))
    return top, bottom


def other_core(x):
    return lax.ppermute(x, "mp", swap(2, 1))


def norm_kernel(down_rows, at, *refs):
    count = 3 if down_rows is None else 4
    sources, held, sems = refs[:count], refs[-1 - count : -1], refs[-1]
    if down_rows is None:
        out_ref = refs[count]
    else:
        weights_ref, out_ref, cut_ref = refs[count : count + 3]
        cutting = pltpu.make_async_copy(
            weights_ref.at[: cut_ref.shape[0], :], cut_ref, sems.at[count]
        )
        cutting.start()
    copies = [
        pltpu.make_async_copy(source, target, sems.at[n])
        for n, (source, target) in enumerate(zip(sources, held))
    ]
    for copy in copies:
        copy.start()
    for copy in copies:
        copy.wait()
    hidden_ref, embed_ref, gain_ref = held[:3]
    hidden = hidden_ref[...].astype(F32)
    embed = embed_ref[...].astype(F32)
    rows, width = hidden.shape
    squares = jnp.sum(hidden * hidden, axis=1, keepdims=True) + jnp.sum(
        embed * embed, axis=1, keepdims=True
    )
    factor = lax.rsqrt(squares / (2 * width) + EPS)

    @pl.when(at[2] == 0)
    def _():
        out_ref[:rows, :] = (hidden * factor * gain_ref[:, :width]).astype(BF16)

    @pl.when(at[2] != 0)
    def _():
        out_ref[:rows, :] = (embed * factor * gain_ref[:, width:]).astype(BF16)

    if down_rows is not None:
        whole = jnp.transpose(held[3][:, :HD].astype(F32)).astype(BF16)
        own = pl.ds(pl.multiple_of(at[0] * down_rows, down_rows), down_rows)
        part = jnp.transpose(held[3][own, HD:].astype(F32)).astype(BF16)
        for x in (whole, part):
            groups = width // x.shape[1]
            step = x.shape[0] // groups
            for g in range(groups):
                columns = slice(g * x.shape[1], (g + 1) * x.shape[1])
                out_ref[rows : rows + step, columns] = x[g * step : (g + 1) * step, :]
            rows += step
        cutting.wait()


def norm(at, hidden, embed, gain, down, down_rows, weights, shard):
    rows, width = hidden.shape
    arrays = (hidden, embed, gain)
    if down_rows is not None:
        arrays += (down,)
        rows += HD * down.shape[0] // width + 2 * HD * down_rows // width
    shapes = [jax.ShapeDtypeStruct((rows, width), BF16)]
    held = [pltpu.VMEM(x.shape, x.dtype) for x in arrays]
    if down_rows is not None:
        arrays += (weights,)
        shapes.append(jax.ShapeDtypeStruct((shard, weights.shape[1]), BF16))
    return pl.pallas_call(
        functools.partial(norm_kernel, down_rows),
        out_shape=shapes,
        in_specs=[pl.BlockSpec(memory_space=SMEM)]
        + [pl.BlockSpec(memory_space=pltpu.MemorySpace.HBM)] * len(arrays),
        out_specs=[pl.BlockSpec(memory_space=pltpu.VMEM)] * len(shapes),
        scratch_shapes=held + [pltpu.SemaphoreType.DMA((len(arrays),))],
        compiler_params=params(60),
        cost_estimate=cost(1, 1),
        name="norm",
    )(at, *arrays)


def arrange_kernel(begin, *refs):
    count = len(refs) - 4
    sources, out_ref, held, sems = refs[:count], refs[-3], refs[-2], refs[-1]
    step, width = held.shape[1:]
    copies = [
        pltpu.make_async_copy(source.at[begin : begin + step, :], held.at[n], sems.at[n])
        for n, source in enumerate(sources)
    ]
    for copy in copies:
        copy.start()
    for copy in copies:
        copy.wait()
    size = out_ref.shape[1] // count
    for n in range(count):
        for g in range(width // size):
            out_ref[g * step : (g + 1) * step, n * size : (n + 1) * size] = held[
                n, :, g * size : (g + 1) * size
            ]


def arrange(blocks, earlier, begin, down_rows):
    width = blocks[0].shape[1]
    step = 2 * HD * down_rows // width
    return pl.pallas_call(
        functools.partial(arrange_kernel, begin),
        out_shape=jax.ShapeDtypeStruct((2 * HD, len(blocks) * down_rows), BF16),
        in_specs=[pl.BlockSpec(memory_space=pl.ANY)] * (len(blocks) + 1),
        out_specs=pl.BlockSpec(memory_space=pltpu.VMEM),
        scratch_shapes=[
            pltpu.VMEM((len(blocks), step, width), BF16),
            pltpu.SemaphoreType.DMA((len(blocks),)),
        ],
        cost_estimate=cost(1, 1),
        name="arrange",
    )(*blocks, earlier)


def project_kernel(plan, stage, at, *refs):
    slots, count, inputs, down_rows = plan
    arrays, outs = refs[:count], refs[count : count + len(inputs)]
    mark, joined, down = refs[count + len(inputs) :]
    mark[0] = jnp.int32(0)
    dp, seq, core = at[0], at[1], at[2]
    rows = joined.shape[0] // len(slots)
    width = joined.shape[1] // 2

    def part(begin, size):
        return pl.ds(pl.multiple_of(begin, size), size)

    if stage == 2:
        half = joined.shape[1]
        columns = part(((dp ^ 3) & 1) * half, half)
        for k, (mine, other) in enumerate(slots):
            joined[part((seq ^ k) * rows, rows), :] = jnp.where(
                (dp ^ 3) >> 1 == core, arrays[mine][:rows, columns], arrays[other][:rows, columns]
            )
        for (index, begun), out in zip(inputs, outs):
            total = arrays[begun][...]
            total += jnp.dot(joined[...], arrays[index][...], preferred_element_type=F32)
            out[...] = total.astype(out.dtype)
        return
    for k, (mine, other) in enumerate(slots):
        at_row = part((seq ^ k) * rows, rows)
        joined[at_row, part(core * width, width)] = arrays[mine][:rows, :]
        joined[at_row, part((1 - core) * width, width)] = arrays[other][:rows, :]
    for n, (_, downs, _) in enumerate(inputs):
        if down_rows is None:
            down[:, n * HD : (n + 1) * HD] = arrays[downs][...]
            continue
        if downs is None:
            size = (joined.shape[1] // 2) // len(slots)
            step = HD * size // width
            for k, pair in enumerate(slots):
                for crossed, index in enumerate(pair):
                    columns = part(((seq ^ k) * 2 + (core ^ crossed)) * size, size)
                    for g in range(width // size):
                        down[g * step : (g + 1) * step, columns] = arrays[index][
                            rows : rows + step, g * size : (g + 1) * size
                        ]
            continue
        for index, row, k, crossed in downs:
            for j in range(4):
                begin = (((seq ^ j) * 2 + (core ^ crossed)) * 4 + (dp ^ k)) * down_rows
                down[n * HD : (n + 1) * HD, part(begin, down_rows)] = arrays[index][
                    row : row + HD, j * down_rows : (j + 1) * down_rows
                ]
    if down_rows is None:
        low = jnp.dot(joined[...], down[...], preferred_element_type=F32).astype(BF16)
    else:
        low = scores_of(joined[...], down[...]).astype(BF16)
    for n, ((weights, _, up), out) in enumerate(zip(inputs, outs)):
        total = jnp.dot(
            low[:, n * HD : (n + 1) * HD], arrays[up][...], preferred_element_type=F32
        )
        for index, row, size, k, start, shard in weights:
            columns = joined[...] if k is None else joined[:, part((dp ^ k) * shard + start, size)]
            total += jnp.dot(columns, arrays[index][row : row + size, :], preferred_element_type=F32)
        out[...] = total.astype(out.dtype)


def project(at, slots, rows, inputs, down_rows, stage=0):
    arrays = []

    def place(array):
        for index, known in enumerate(arrays):
            if known is array:
                return index
        arrays.append(array)
        return len(arrays) - 1

    placed = tuple(tuple(place(x) for x in slot) for slot in slots)
    plans = []
    for weights, downs, up in inputs:
        weights = tuple((place(piece[0]), *piece[1:]) for piece in weights)
        if down_rows is None:
            downs = place(downs)
        elif downs is not None:
            downs = tuple((place(piece[0]), *piece[1:]) for piece in downs)
        plans.append((weights, downs, place(up)))
    width = 2 * slots[0][0].shape[1]
    columns = inputs[0][2].shape[1]
    result = jax.ShapeDtypeStruct((rows, columns), F32 if stage == 1 else BF16)
    ranks = len(inputs) * HD
    return pl.pallas_call(
        functools.partial(project_kernel, (placed, len(arrays), tuple(plans), down_rows), stage),
        out_shape=(*(result,) * len(inputs), MARK),
        in_specs=[pl.BlockSpec(memory_space=SMEM)]
        + [pl.BlockSpec(memory_space=pltpu.VMEM)] * len(arrays),
        out_specs=(
            *(pl.BlockSpec(memory_space=pltpu.VMEM),) * len(inputs),
            pl.BlockSpec(memory_space=SMEM),
        ),
        scratch_shapes=[
            pltpu.VMEM((rows, width), BF16),
            pltpu.VMEM((width, ranks) if down_rows is None else (ranks, width), BF16),
        ],
        compiler_params=params((18 if len(inputs) == 1 else 28) if down_rows is not None else 40),
        cost_estimate=cost(
            2 * rows * width * (columns + HD) * len(inputs), 2 * width * (rows + columns * len(inputs))
        ),
        name="project",
    )(at, *arrays)


def project_rest(at, slots, rows, last, begun, *earlier):
    arrays = [x for slot in slots for x in slot] + [*last, *begun, *earlier]
    count = len(arrays) - len(earlier)
    placed = tuple((2 * k, 2 * k + 1) for k in range(len(slots)))
    first = 2 * len(slots)
    plans = tuple((first + n, first + len(last) + n) for n in range(len(last)))
    result = jax.ShapeDtypeStruct(begun[0].shape, BF16)
    return pl.pallas_call(
        functools.partial(project_kernel, (placed, len(arrays), plans, None), 2),
        out_shape=(*(result,) * len(last), MARK),
        in_specs=[pl.BlockSpec(memory_space=SMEM)]
        + [pl.BlockSpec(memory_space=pltpu.VMEM)] * count
        + [pl.BlockSpec(memory_space=pl.ANY)] * len(earlier),
        out_specs=(
            *(pl.BlockSpec(memory_space=pltpu.VMEM),) * len(last),
            pl.BlockSpec(memory_space=SMEM),
        ),
        scratch_shapes=[
            pltpu.VMEM((rows, last[0].shape[0]), BF16),
            pltpu.VMEM((8, HD), BF16),
        ],
        compiler_params=params(18),
        cost_estimate=cost(1, 1),
        name="project_rest",
    )(at, *arrays)


def finish_head(head, heads, weighted, peak, total, out_ref, stats):
    level = peak + jnp.log(total)
    high = level.astype(BF16).astype(F32)
    rest = level - high
    mid = rest.astype(BF16).astype(F32)
    stats[3 * head : 3 * head + 1, :] = high
    stats[3 * head + 1 : 3 * head + 2, :] = mid
    stats[3 * head + 2 : 3 * head + 3, :] = rest - mid
    out_ref[head * HD : (head + 1) * HD, :] = (weighted / total).astype(BF16)
    if head == heads - 1:
        out_ref[heads * HD :, :] = stats[...].astype(BF16)


def over_keys(left, right):
    return lax.dot_general(left, right, (((0,), (0,)), ((), ())), preferred_element_type=F32)


def scores_of(keys, queries):
    return lax.dot_general(keys, queries, (((1,), (1,)), ((), ())), preferred_element_type=F32)


def cache_kernel(
    slot,
    heads,
    at,
    earlier,
    pages,
    query_ref,
    key_ref,
    value_ref,
    shared_key_ref,
    shared_value_ref,
    out_ref,
    mark,
    stats,
):
    mark[0] = jnp.int32(0)
    stats[...] = jnp.zeros_like(stats)
    scale = 1.0 / math.sqrt(HD)
    group = at[4]
    for head in range(heads):
        columns = pl.ds(pl.multiple_of(((at[1] ^ slot) * heads + head) * HD, HD), HD)
        queries = query_ref[:, head * HD : (head + 1) * HD]
        own = scores_of(key_ref[0, :, columns], queries) * scale
        shared = scores_of(shared_key_ref[group, :, columns], queries) * scale
        offset = lax.broadcasted_iota(jnp.int32, (PAGE, own.shape[1]), 0)
        masked = []
        for u in range(own.shape[0] // PAGE):
            usable = offset < at[3] - pages[u] * PAGE
            masked.append(jnp.where(usable, own[u * PAGE : (u + 1) * PAGE], NEG))
        own = jnp.concatenate(masked, axis=0)
        peak = jnp.maximum(
            jnp.max(own, axis=0, keepdims=True), jnp.max(shared, axis=0, keepdims=True)
        )
        own = jnp.exp(own - peak)
        shared = jnp.exp(shared - peak)
        total = jnp.sum(own, axis=0, keepdims=True) + jnp.sum(shared, axis=0, keepdims=True)
        weighted = over_keys(value_ref[0, :, columns], own.astype(BF16)) + over_keys(
            shared_value_ref[group, :, columns], shared.astype(BF16)
        )
        finish_head(head, heads, weighted, peak, total, out_ref, stats)


def cache_attention(at, earlier, pages, slot, queries, own_keys, own_values, shared_keys, shared_values):
    rows, width = queries.shape
    heads = width // HD
    slots, shared_slots = own_keys.shape[1], shared_keys.shape[1]
    return pl.pallas_call(
        functools.partial(cache_kernel, slot, heads),
        out_shape=(jax.ShapeDtypeStruct((width + STAT_ROWS, rows), BF16), MARK),
        in_specs=[pl.BlockSpec(memory_space=SMEM)] * 3
        + [pl.BlockSpec(memory_space=pltpu.VMEM)] * 5,
        out_specs=(pl.BlockSpec(memory_space=pltpu.VMEM), pl.BlockSpec(memory_space=SMEM)),
        scratch_shapes=[pltpu.VMEM((STAT_ROWS, rows), F32)],
        compiler_params=params(16),
        cost_estimate=cost(
            8 * rows * width * (slots + shared_slots),
            4 * width * (slots + shared_slots),
            rows * heads * (slots + shared_slots),
        ),
        name="cache_attention",
    )(at, earlier, pages, queries, own_keys, own_values, shared_keys, shared_values)


def new_kernel(heads, query_ref, key_ref, value_ref, out_ref, stats):
    stats[...] = jnp.zeros_like(stats)
    for head in range(heads):
        columns = slice(head * HD, (head + 1) * HD)
        scores = scores_of(key_ref[:, columns], query_ref[:, columns]) * (1.0 / math.sqrt(HD))
        places = lax.broadcasted_iota(jnp.int32, scores.shape, 0)
        tokens = lax.broadcasted_iota(jnp.int32, scores.shape, 1)
        scores = jnp.where(places <= tokens, scores, NEG)
        peak = jnp.max(scores, axis=0, keepdims=True)
        exponent = jnp.exp(scores - peak)
        total = jnp.sum(exponent, axis=0, keepdims=True)
        weighted = over_keys(value_ref[:, columns], exponent.astype(BF16))
        finish_head(head, heads, weighted, peak, total, out_ref, stats)


def new_attention(queries, keys, values):
    rows, width = queries.shape
    heads = width // HD
    return pl.pallas_call(
        functools.partial(new_kernel, heads),
        out_shape=jax.ShapeDtypeStruct((width + STAT_ROWS, rows), BF16),
        in_specs=[pl.BlockSpec(memory_space=pltpu.VMEM)] * 3,
        out_specs=pl.BlockSpec(memory_space=pltpu.VMEM),
        scratch_shapes=[pltpu.VMEM((STAT_ROWS, rows), F32)],
        compiler_params=params(10),
        cost_estimate=cost(8 * rows * rows * width, 8 * rows * width, rows * rows * heads),
        name="new_attention",
    )(queries, keys, values)


def merge_kernel(heads, blocks, at, *refs):
    parts = refs[: len(refs) - 3]
    keep_ref, give_ref, attended = refs[len(refs) - 3 :]
    base = heads * HD
    for h in range(heads):
        levels = []
        for part in parts:
            stats = part[base : base + STAT_ROWS, :].astype(F32)
            levels.append(
                stats[3 * h : 3 * h + 1] + (stats[3 * h + 1 : 3 * h + 2] + stats[3 * h + 2 : 3 * h + 3])
            )
        highest = functools.reduce(jnp.maximum, levels)
        weights = [jnp.exp(level - highest) for level in levels]
        mass = functools.reduce(jnp.add, weights)
        joined = functools.reduce(
            jnp.add,
            [w * part[h * HD : (h + 1) * HD, :].astype(F32) for w, part in zip(weights, parts)],
        )
        attended[:, h * HD : (h + 1) * HD] = jnp.transpose(joined / mass)
    step = keep_ref.shape[0] // blocks
    for block in range(blocks):
        here = pl.ds(pl.multiple_of((2 * block + at[2]) * step, step), step)
        there = pl.ds(pl.multiple_of((2 * block + 1 - at[2]) * step, step), step)
        keep_ref[block * step : (block + 1) * step, :] = attended[here, :].astype(BF16)
        give_ref[block * step : (block + 1) * step, :] = attended[there, :].astype(BF16)


def merge(at, parts, blocks):
    rows = parts[0].shape[1]
    width = parts[0].shape[0] - STAT_ROWS
    half = jax.ShapeDtypeStruct((rows // 2, width), BF16)
    return pl.pallas_call(
        functools.partial(merge_kernel, width // HD, blocks),
        out_shape=(half, half),
        in_specs=[pl.BlockSpec(memory_space=SMEM)]
        + [pl.BlockSpec(memory_space=pltpu.VMEM)] * len(parts),
        out_specs=(pl.BlockSpec(memory_space=pltpu.VMEM),) * 2,
        scratch_shapes=[pltpu.VMEM((rows, width), F32)],
        compiler_params=params(),
        cost_estimate=cost(1, 1),
        name="merge",
    )(at, *parts)


def output_kernel(count, blocks, at, keep_ref, got_ref, *refs):
    mine, other = refs[:count], refs[count : len(refs) - blocks - 1]
    outs, total = refs[-1 - blocks : -1], refs[-1]
    depth = keep_ref.shape[1]
    groups = 4 if count == 5 else 1
    width = total.shape[1] // groups
    for k in range(groups):
        if k < 3:
            here = jnp.dot(keep_ref[...], mine[k][:depth, :], preferred_element_type=F32)
            there = other[0][k * depth : (k + 1) * depth, :]
        else:
            half = depth // 2
            here = jnp.dot(keep_ref[:, :half], mine[3][:half, :], preferred_element_type=F32)
            here += jnp.dot(keep_ref[:, half:], mine[4][...], preferred_element_type=F32)
            there = other[1][...]
        here += jnp.dot(got_ref[...], there, preferred_element_type=F32)
        total[:, k * width : (k + 1) * width] = here
    step = total.shape[0] // blocks
    for k in range(blocks):
        at_row = pl.ds(pl.multiple_of((at[1] ^ k) * step, step), step)
        outs[k][...] = total[at_row, :].astype(BF16)


def output_projection(at, keep, got, mine, other, blocks):
    columns = mine[0].shape[1] * (4 if len(mine) == 5 else 1)
    block = jax.ShapeDtypeStruct((keep.shape[0] // blocks, columns), BF16)
    return pl.pallas_call(
        functools.partial(output_kernel, len(mine), blocks),
        out_shape=(block,) * blocks,
        in_specs=[pl.BlockSpec(memory_space=SMEM)]
        + [pl.BlockSpec(memory_space=pltpu.VMEM)] * (2 + len(mine) + len(other)),
        out_specs=(pl.BlockSpec(memory_space=pltpu.VMEM),) * blocks,
        scratch_shapes=[pltpu.VMEM((keep.shape[0], columns), F32)],
        compiler_params=params(20),
        cost_estimate=cost(1, 1),
        name="output_projection",
    )(at, keep, got, *mine, *other)


def sum_kernel(groups, at, mask_ref, *refs):
    parts, out_ref = refs[:-1], refs[-1]
    width = out_ref.shape[1] // groups
    mask = mask_ref[:, :1]
    for k in range(groups):
        here = slice(k * width, (k + 1) * width)
        total = functools.reduce(jnp.add, [part[:, here].astype(F32) for part in parts])
        total = total * mask
        if groups == 1:
            out_ref[...] = total.astype(BF16)
        else:
            begin = pl.multiple_of((at[0] ^ k) * width, width)
            out_ref[:, pl.ds(begin, width)] = total.astype(BF16)


def final_sum(at, mask, parts, groups):
    return pl.pallas_call(
        functools.partial(sum_kernel, groups),
        out_shape=jax.ShapeDtypeStruct(parts[0].shape, BF16),
        in_specs=[pl.BlockSpec(memory_space=SMEM)]
        + [pl.BlockSpec(memory_space=pltpu.VMEM)] * (1 + len(parts)),
        out_specs=pl.BlockSpec(memory_space=pltpu.VMEM),
        compiler_params=params(),
        cost_estimate=cost(1, 1),
        name="final_sum",
    )(at, mask, *parts)


def query_4(at, blocks, rows, weights, up, down_rows, *gate):
    shard = weights.shape[0]
    half = shard // 2
    by_x, by_y = both_ways(weights)
    top, bottom = halves_on(by_x, by_y, None, *gate)
    pieces = [(x, 0, shard, k, 0, shard) for k, x in enumerate((weights, by_x, by_y))]
    pieces += [(top, 0, half, 3, 0, shard), (bottom, 0, half, 3, half, shard)]
    query, mark = project(at, blocks, rows, [(pieces, None, up)], down_rows)
    return query, mark, [top, bottom]


def begin_4(at, blocks, rows, weights, near, downs, ups, down_rows):
    shard = weights.shape[0] // 2
    other = other_core(assemble([(x, row, 2 * HD) for x, row in downs]))
    inputs = []
    for n in range(2):
        pieces = [(x, n * shard, shard, k, 0, shard) for k, x in enumerate((weights, *near))]
        small = [(x, row + n * HD, k, 0) for k, (x, row) in enumerate(downs)]
        small += [(other, (2 * k + n) * HD, k, 1) for k in range(4)]
        inputs.append((pieces, small, ups[n]))
    return project(at, blocks, rows, inputs, down_rows, 1)[:2]


def shards(
    hidden_states,
    embeddings,
    norm_gain,
    input_weights,
    adapter_down,
    adapter_up,
    output_weights,
    own_keys,
    own_values,
    shared_keys,
    shared_values,
    cached_lengths,
    prompt_group,
    slot_pages,
    padding_mask,
):
    dp, seq, mp = (lax.axis_index(axis) for axis in ("dp", "seq", "mp"))
    seq_count = lax.axis_size("seq")
    by_four = lax.axis_size("dp") == 4 and seq_count == 4
    at = jnp.stack([dp, seq, mp, cached_lengths[0], prompt_group[0]])
    pages = slot_pages[0]
    ups = [adapter_up[p, :, 0] for p in range(3)]
    down_rows = adapter_down.shape[0] // 4

    own_rows = hidden_states.shape[0]
    rows = own_rows * seq_count
    shard, _, _, width = input_weights.shape
    own_weights = jnp.transpose(input_weights[:, :, 0], (1, 0, 2)).reshape(-1, width)
    half, *weights = norm(
        at,
        hidden_states,
        embeddings,
        norm_gain[None, :],
        adapter_down,
        down_rows if by_four else None,
        own_weights,
        shard,
    )
    mine = spread(half)
    blocks = [(block, other_core(block)) for block in mine]
    if by_four:
        weights = weights[0]
        query, mark, arrived = query_4(at, blocks, rows, weights, ups[0], down_rows, mine[2])
    else:
        whole = lax.all_gather(input_weights[:, :, 0], "dp", axis=0, tiled=True)
        down = lax.all_gather(adapter_down, ("seq", "mp"), axis=0, tiled=True)
        inputs = [
            ([(whole[:, p], 0, whole.shape[0], None, 0, 0)], down[:, p * HD : (p + 1) * HD], ups[p])
            for p in range(3)
        ]
        query, key, value, mark = project(at, blocks, rows, inputs, None)
    queries = spread(query)

    parts, sent, marks = {}, {}, [mark]
    for k in range(seq_count):
        parts[k], mark = cache_attention(
            at,
            marks[-1],
            pages,
            k,
            queries[k],
            own_keys,
            own_values,
            shared_keys,
            shared_values,
        )
        marks.append(mark)
        sent[k] = lax.ppermute(parts[k], "seq", swap(seq_count, k)) if k else parts[k]

    if by_four:
        begin = own_rows + HD * adapter_down.shape[0] // half.shape[1]
        down = arrange(mine, marks[0], begin, down_rows)
        exchanged = [block[1] for block in blocks[:3]]
        weights = cut(own_weights, shard, 2 * shard, mine[3], *exchanged, *arrived)
        near = both_ways(weights)
        far = lax.ppermute(down, "dp", swap(4, 3))
        depth = output_weights.shape[1]
        output_own = assemble(
            [(output_weights[0], 0, depth), (down, 0, 2 * HD)], *near, far, marks[3]
        )
        by_x, by_y = both_ways(output_own)
        downs = [(down, 0), (by_x, depth), (by_y, depth), (far, 0)]
        begun = begin_4(at, blocks, rows, weights, near, downs, ups[1:], down_rows)
        top = along_y(assemble([(by_x, 0, depth // 2)]))
        bottom = along_x(assemble([(by_y, depth // 2, depth // 2)]))
        last = halves_on(*near, None, queries[3], sent[2], top, bottom)
        key, value, _ = project_rest(at, blocks, rows, last, begun, sent[1], sent[3])
        out_mine = [output_own, by_x, by_y, top, bottom]
        out_other = [
            other_core(assemble([(x, 0, size) for x in part]))
            for part, size in ((out_mine[:3], depth), (out_mine[3:], depth // 2))
        ]
    else:
        out_mine = [lax.all_gather(output_weights[0], "dp", axis=1, tiled=True)]
        out_other = [other_core(out_mine[0])]

    joined = [sent[k] for k in range(seq_count)] + [new_attention(query, key, value)]
    keep, give = merge(at, joined, seq_count)
    got = other_core(give)
    sums = output_projection(at, keep, got, out_mine, out_other, seq_count)
    sums = [sums[0]] + [lax.ppermute(sums[k], "seq", swap(seq_count, k)) for k in range(1, seq_count)]
    mask = jnp.broadcast_to(padding_mask.astype(F32)[:, None], (padding_mask.shape[0], HD))
    return final_sum(at, mask, sums, 4 if by_four else 1)


def solution(mesh):
    placed = (
        P(("dp", "seq"), None),
        P(("dp", "seq"), None),
        P(),
        P("dp", None, "mp", "seq"),
        P(("seq", "mp"), None),
        P(None, None, "mp", "seq"),
        P("mp", "seq", "dp"),
        P("dp", "seq", "mp"),
        P("dp", "seq", "mp"),
        P(None, "seq", "mp"),
        P(None, "seq", "mp"),
        P("dp"),
        P("dp"),
        P("dp", "seq"),
        P(("dp", "seq", "mp")),
    )
    return jax.shard_map(
        shards, mesh=mesh, in_specs=placed, out_specs=P(("dp", "seq", "mp"), None), check_vma=False
    )
```
